128 devices in a mesh: ctx: 64 (over x_lo, y, z, core), sec: 2 (over x_hi).
Axes of the slice: x: 4 (x_hi: 2, x_lo: 2; x = x_hi * 2 + x_lo), y: 4, z: 4, core: 2. Of those that a mesh axis runs over, the one named last changes fastest.
Arguments:
- query_nope: bfloat16 [4096, 8192], P('ctx', 'sec'), may hold values from -6 to 6
- query_rope: bfloat16 [4096, 4096], P('ctx', 'sec'), may hold values from -8 to 8
- key_latent: bfloat16 [4096, 512], P('ctx'), may hold values from -6 to 6
- key_rope: bfloat16 [4096, 64], P('ctx'), may hold values from -8 to 8
- key_up: bfloat16 [64, 512, 128], P('sec'), may hold values from -0.25 to 0.25
- value_up: bfloat16 [64, 512, 128], P('sec'), may hold values from -1 to 1
- routed_tokens: bfloat16 [16384, 7168], P(('ctx', 'sec')), may hold values from -6 to 6
- expert_ids: int32 [16384, 8], P(('ctx', 'sec')), may hold values from 0 to 255, as said below
- expert_gates: float32 [16384, 8], P(('ctx', 'sec')), may hold values from 0.2 to 2
- gate_weight: bfloat16 [7168, 32768], P(None, ('ctx', 'sec')), may hold values from -0.0625 to 0.0625
- up_weight: bfloat16 [7168, 32768], P(None, ('ctx', 'sec')), may hold values from -0.0625 to 0.0625
- down_weight: bfloat16 [32768, 7168], P(('ctx', 'sec')), may hold values from -0.125 to 0.125
Outputs:
- attention_out: bfloat16 [4096, 8192], P('ctx', 'sec')
- routed_out: bfloat16 [16384, 7168], P(('ctx', 'sec'))
The draws below stay inside these ranges and needn't reach their ends.
Inputs may be any that keep to these rules, and one draw needn't show every extreme that they name: `expert_ids`: each row names 8 different experts, at most one of them below 16. Within each aligned block of 128 rows (the rows of one device) no expert below 16 is named more than 4 times, and in every draw one expert below 16 is named exactly 4 times in every block.
All inputs are finite; a program needn't handle non-finite values.
Results may differ from the reference program's by a relative error of at most 0.008.
Values may be sent and summed in bfloat16 or wider, within the bound.
No kernel may reach another device: no remote copies, remote signals or barrier semaphores. Data moves between devices by JAX's collectives and lax.ppermute only.
A program may use at most 192 MiB of HBM per device.

```python
import jax
import jax.numpy as jnp
from jax import lax

D = 7168
FF = 2048
EXPERTS = 256
TOPK = 8
LAT = 512
ROPE = 64
NOPE = 128
VDIM = 128
HEADS = 64
CAP = 4
MTOK_DEV = 128
EXP_ROUND = 16
SEQ = 4096
MTOKENS = 16384
ROUND_FF = 32768
N_CTX = 64
N_SEC = 2


def draw_query_rope(key, part):
    array_shape = (SEQ, HEADS * ROPE)
    values = jnp.clip(jax.random.normal(jax.random.fold_in(key, 1), array_shape, jnp.float32), -6.0, 6.0)
    return values.astype(jnp.bfloat16)


def draw_key_rope(key, part):
    array_shape = (SEQ, ROPE)
    values = jnp.clip(jax.random.normal(jax.random.fold_in(key, 2), array_shape, jnp.float32), -6.0, 6.0)
    return values.astype(jnp.bfloat16)


def draw_expert_ids(key, part):
    block_count = MTOKENS // MTOK_DEV
    outside_count = EXPERTS - EXP_ROUND
    scores = jax.random.randint(jax.random.fold_in(key, 1), (MTOKENS, outside_count), 0, 1 << 20)
    scores = scores * outside_count + jnp.arange(outside_count, dtype=jnp.int32)[None, :]
    picked = lax.top_k(scores, TOPK)[1].astype(jnp.int32) + EXP_ROUND
    levels = jax.random.randint(jax.random.fold_in(key, 2), (EXP_ROUND,), 1, 5)
    hot_expert = jax.random.randint(jax.random.fold_in(key, 3), (), 0, EXP_ROUND)
    counts = jax.random.randint(jax.random.fold_in(key, 4), (block_count, EXP_ROUND), 0, levels * CAP // 4 + 1)
    expert_range = jnp.arange(EXP_ROUND, dtype=jnp.int32)
    counts = jnp.where(expert_range[None, :] == hot_expert, CAP, counts)
    starts = jnp.cumsum(counts, axis=1) - counts
    block_keys = jax.random.split(jax.random.fold_in(key, 5), block_count)
    rank_rows = jax.vmap(lambda block_key: jax.random.permutation(block_key, MTOK_DEV))(block_keys)
    inside = (rank_rows[:, :, None] >= starts[:, None, :]) & (rank_rows[:, :, None] < (starts + counts)[:, None, :])
    member = jnp.any(inside, axis=2).reshape(MTOKENS)
    chosen = jnp.sum(jnp.where(inside, expert_range[None, None, :], 0), axis=2).reshape(MTOKENS)
    column = jax.random.randint(jax.random.fold_in(key, 6), (MTOKENS,), 0, TOPK)
    replace = member[:, None] & (jnp.arange(TOPK, dtype=jnp.int32)[None, :] == column[:, None])
    return jnp.where(replace, chosen[:, None], picked).astype(jnp.int32)


def steps_of(key, extent, shards, smallest, top_value):
    def one(dim, parts):
        heights = jax.random.uniform(jax.random.fold_in(jax.random.fold_in(key, 6), dim), (parts,), jnp.float32, smallest / len(shards), top_value / len(shards))
        return jnp.repeat(jnp.exp(heights), extent[dim] // parts).reshape((-1,) + (1,) * (len(extent) - dim - 1))

    gain = one(*shards[0])
    for cut in shards[1:]:
        gain = gain * one(*cut)
    return gain


def normal_values(rng, extent, width, limit, pieces=(), kind=jnp.bfloat16):
    array = jax.random.normal(rng, extent, jnp.float32) * width
    if len(pieces) > 0:
        array = steps_of(rng, extent, pieces, -0.22, 0.18) * array
    return jnp.clip(array, min=-limit, max=limit).astype(kind)


def setup_inputs(seed: int = 0) -> dict:
    streams_of = jax.random.split(jax.random.key(seed), 13)
    return {
        "query_nope": normal_values(streams_of[0], (SEQ, HEADS * NOPE), 1.0, 6.0, ((0, 64), (1, 2))),
        "query_rope": draw_query_rope(jax.random.fold_in(streams_of[12], 71), 0),
        "key_latent": normal_values(streams_of[2], (SEQ, LAT), 1.0, 6.0, ((0, 64),)),
        "key_rope": draw_key_rope(jax.random.fold_in(streams_of[12], 71), 0),
        "key_up": normal_values(streams_of[4], (HEADS, LAT, NOPE), LAT ** -0.5, 0.25, ((0, 2),)),
        "value_up": normal_values(streams_of[5], (HEADS, LAT, VDIM), (LAT // 16) ** -0.5, 1.0, ((0, 2),)),
        "routed_tokens": normal_values(streams_of[6], (MTOKENS, D), 1.0, 6.0, ((0, 128),)),
        "expert_ids": draw_expert_ids(jax.random.fold_in(streams_of[12], 71), 0),
        "expert_gates": jnp.clip(0.2 + 1.8 * jax.random.uniform(streams_of[8], (MTOKENS, TOPK), jnp.float32) ** steps_of(streams_of[8], (MTOKENS, TOPK), ((0, 128),), -0.2, 0.2), 0.2, 2.0),
        "gate_weight": normal_values(streams_of[9], (D, ROUND_FF), D ** -0.5, 0.0625, ((1, 128),)),
        "up_weight": normal_values(streams_of[10], (D, ROUND_FF), D ** -0.5, 0.0625, ((1, 128),)),
        "down_weight": normal_values(streams_of[11], (ROUND_FF, D), FF ** -0.5, 0.125, ((0, 128),)),
    }


def head_attention(query_latent, query_rotary, key_latent, key_rope, value_map):
    score_scale = (NOPE + ROPE) ** -0.5
    scores = jnp.dot(query_latent, key_latent.T, preferred_element_type=jnp.float32)
    scores = (scores + jnp.dot(query_rotary, key_rope.T, preferred_element_type=jnp.float32)) * score_scale
    places = jnp.arange(SEQ, dtype=jnp.int32)
    allowed = places[None, :] <= places[:, None]
    scores = jnp.where(allowed, scores, -jnp.inf)
    row_max = jnp.max(scores, axis=1, keepdims=True)
    exponent = jnp.where(allowed, jnp.exp(scores - row_max), 0.0)
    row_sum = jnp.sum(exponent, axis=1, keepdims=True)
    weights = exponent.astype(jnp.bfloat16)
    latent_out = (jnp.dot(weights, key_latent, preferred_element_type=jnp.float32) / row_sum).astype(jnp.bfloat16)
    return jnp.dot(latent_out, value_map, preferred_element_type=jnp.float32).astype(jnp.bfloat16)


def attention(query_nope, query_rope, key_latent, key_rope, key_up, value_up):
    nope_heads = query_nope.reshape(SEQ, HEADS, NOPE)
    rope_heads = query_rope.reshape(SEQ, HEADS, ROPE)

    def one_head(head_index):
        query_latent = jnp.dot(nope_heads[:, head_index, :], key_up[head_index].T, preferred_element_type=jnp.float32).astype(jnp.bfloat16)
        return head_attention(query_latent, rope_heads[:, head_index, :], key_latent, key_rope, value_up[head_index])

    per_head = lax.map(one_head, jnp.arange(HEADS, dtype=jnp.int32))
    return jnp.transpose(per_head, (1, 0, 2)).reshape(SEQ, HEADS * VDIM)


def routed_experts(routed_tokens, expert_ids, expert_gates, gate_weight, up_weight, down_weight):
    budget_rows = N_CTX * N_SEC * CAP
    slot_places = jnp.arange(budget_rows, dtype=jnp.int32)

    def one_expert(summed, expert):
        chosen = expert_ids == expert
        is_named = jnp.any(chosen, axis=1)
        coefficient = jnp.sum(jnp.where(chosen, expert_gates, 0.0), axis=1)
        named_count = jnp.sum(is_named.astype(jnp.int32))
        token_index = jnp.nonzero(is_named, size=budget_rows, fill_value=0)[0].astype(jnp.int32)
        picked_rows = routed_tokens[token_index]
        column_start = expert * FF
        gate_cols = lax.dynamic_slice_in_dim(gate_weight, column_start, FF, 1)
        up_cols = lax.dynamic_slice_in_dim(up_weight, column_start, FF, 1)
        down_rows = lax.dynamic_slice_in_dim(down_weight, column_start, FF, 0)
        gate_act = jnp.dot(picked_rows, gate_cols, preferred_element_type=jnp.float32)
        up_act = jnp.dot(picked_rows, up_cols, preferred_element_type=jnp.float32)
        hidden = (jax.nn.silu(gate_act) * up_act).astype(jnp.bfloat16)
        expert_out = jnp.dot(hidden, down_rows, preferred_element_type=jnp.float32)
        row_scale = jnp.where(slot_places < named_count, coefficient[token_index], 0.0)
        return summed.at[token_index].add(row_scale[:, None] * expert_out), None

    start_sum = jnp.zeros((MTOKENS, D), jnp.float32)
    summed, _ = lax.scan(one_expert, start_sum, jnp.arange(EXP_ROUND, dtype=jnp.int32))
    return summed.astype(jnp.bfloat16)


def reference(query_nope, query_rope, key_latent, key_rope, key_up, value_up, routed_tokens, expert_ids, expert_gates, gate_weight, up_weight, down_weight):
    attention_out = attention(query_nope, query_rope, key_latent, key_rope, key_up, value_up)
    routed_out = routed_experts(routed_tokens, expert_ids, expert_gates, gate_weight, up_weight, down_weight)
    return (attention_out, routed_out)
```

```python
import functools

import jax
import jax.numpy as jnp
from jax import lax
from jax.experimental import pallas as pl
from jax.experimental.pallas import tpu as pltpu
from jax.sharding import Mesh
from jax.sharding import PartitionSpec as P

AXES = ("xl", "y", "zh", "zl", "core", "sec")
CTX = ("xl", "y", "zh", "zl", "core")
CHIPS = ("xl", "y", "zh", "zl", "sec")
ROPE = 64
NOPE = 128
LAT = 512
KW = 640
CAP = 4
NEXP = 16
HALF = 3584
CB = 512
NCB = HALF // CB
MB = 1024 * 1024
bf16 = jnp.bfloat16
f32 = jnp.float32


def swap_core(x):
    return lax.ppermute(x, "core", [(0, 1), (1, 0)])


def slot_select(ids, gates, side, paired):
    tokens = ids.shape[0]
    slots = NEXP * CAP * (2 if paired else 1)
    col = lax.broadcasted_iota(jnp.int32, (tokens, slots), 1)
    expert = col // 8 if paired else col // 4
    named = jnp.zeros((tokens, slots), f32)
    for k in range(ids.shape[1]):
        named = named + jnp.where(ids[:, k : k + 1] == expert, 1.0, 0.0)
    row_i = lax.broadcasted_iota(jnp.int32, (tokens, tokens), 0)
    col_i = lax.broadcasted_iota(jnp.int32, (tokens, tokens), 1)
    before = jnp.where(col_i < row_i, 1.0, 0.0).astype(bf16)
    rank = jnp.dot(before, named.astype(bf16), preferred_element_type=f32)
    hit = jnp.logical_and(named > 0.5, rank == (col % 4).astype(f32))
    if paired:
        hit = jnp.logical_and(hit, (col // 4) % 2 == side)
    gate = None
    if gates is not None:
        gate = jnp.sum(jnp.where(ids < NEXP, gates, 0.0), axis=1, keepdims=True)
    return jnp.where(hit, 1.0, 0.0), gate


def pack_kernel(c_ref, ids_own, ids_sib, tok_own, tok_sib, out_ref, sel_own, sel_sib):
    c = c_ref[0]

    @pl.when(pl.program_id(0) == 0)
    def _():
        own, _g = slot_select(ids_own[...], None, c, True)
        sib, _h = slot_select(ids_sib[...], None, 1 - c, True)
        sel_own[...] = own.T.astype(bf16)
        sel_sib[...] = sib.T.astype(bf16)

    rows = jnp.dot(sel_own[...], tok_own[...], preferred_element_type=f32)
    rows = rows + jnp.dot(sel_sib[...], tok_sib[...], preferred_element_type=f32)
    rows = rows.astype(bf16).reshape(NEXP, 1, 2 * CAP, CB)
    out_ref[...] = jnp.broadcast_to(rows, (NEXP, 4, 2 * CAP, CB)).reshape(4 * NEXP, 2 * CAP, CB)


def pack_rows(core, ids_own, ids_sib, tokens, tok_sib):
    n = tokens.shape[0]
    return pl.pallas_call(
        pack_kernel,
        grid_spec=pltpu.PrefetchScalarGridSpec(
            num_scalar_prefetch=1,
            grid=(NCB,),
            in_specs=[
                pl.BlockSpec((n, 8), lambda i, c: (0, 0)),
                pl.BlockSpec((n, 8), lambda i, c: (0, 0)),
                pl.BlockSpec((n, CB), lambda i, c: (0, c[0] * NCB + i)),
                pl.BlockSpec((n, CB), lambda i, c: (0, i)),
            ],
            out_specs=pl.BlockSpec((4 * NEXP, 2 * CAP, CB), lambda i, c: (0, 0, i)),
            scratch_shapes=[pltpu.VMEM((128, n), bf16), pltpu.VMEM((128, n), bf16)],
        ),
        out_shape=jax.ShapeDtypeStruct((4 * NEXP, 2 * CAP, HALF), bf16),
        compiler_params=pltpu.CompilerParams(vmem_limit_bytes=16 * MB),
        cost_estimate=pl.CostEstimate(flops=2 * 128 * 256 * HALF, bytes_accessed=6 * MB, transcendentals=0),
    )(core, ids_own, ids_sib, tokens, tok_sib)


def gate_up_kernel(c_ref, x_ref, wg_ref, wu_ref, out_ref):
    x = x_ref[...]
    g = jnp.dot(x, wg_ref[...], preferred_element_type=f32)
    u = jnp.dot(x, wu_ref[...], preferred_element_type=f32)

    @pl.when(pl.program_id(0) == 0)
    def _():
        out_ref[:, :256] = g
        out_ref[:, 256:] = u

    @pl.when(pl.program_id(0) > 0)
    def _():
        out_ref[:, :256] += g
        out_ref[:, 256:] += u


def gate_up(core, x, wg, wu):
    rows = x.shape[0]
    whole = wg.shape[0] == 2 * HALF
    wmap = (lambda i, c: (c[0] * NCB + i, 0)) if whole else (lambda i, c: (i, 0))
    return pl.pallas_call(
        gate_up_kernel,
        grid_spec=pltpu.PrefetchScalarGridSpec(
            num_scalar_prefetch=1,
            grid=(NCB,),
            in_specs=[
                pl.BlockSpec((rows, CB), lambda i, c: (0, i)),
                pl.BlockSpec((CB, 256), wmap),
                pl.BlockSpec((CB, 256), wmap),
            ],
            out_specs=pl.BlockSpec((rows, 512), lambda i, c: (0, 0)),
        ),
        out_shape=jax.ShapeDtypeStruct((rows, 512), f32),
        compiler_params=pltpu.CompilerParams(vmem_limit_bytes=16 * MB),
        cost_estimate=pl.CostEstimate(flops=2 * rows * HALF * 512, bytes_accessed=8 * MB, transcendentals=0),
    )(core, x, wg, wu)


def down_kernel(c_ref, own_ref, own_add, sib_ref, sib_add, wd_ref, wr_ref, out_ref, h_own, h_sib):
    @pl.when(pl.program_id(0) == 0)
    def _():
        for a, b, h in ((own_ref, own_add, h_own), (sib_ref, sib_add, h_sib)):
            g = a[:, :256] + b[:, :256]
            u = a[:, 256:] + b[:, 256:]
            h[...] = (g / (1.0 + jnp.exp(-g)) * u).astype(bf16)

    y = jnp.dot(h_own[...], wd_ref[...], preferred_element_type=f32)
    y = y + jnp.dot(h_sib[...], wr_ref[...], preferred_element_type=f32)
    out_ref[...] = y.astype(bf16)


def down(core, own, own_add, sib, sib_add, wd, wr):
    rows = own.shape[0]
    full = lambda i, c: (0, 0)
    return pl.pallas_call(
        down_kernel,
        grid_spec=pltpu.PrefetchScalarGridSpec(
            num_scalar_prefetch=1,
            grid=(NCB,),
            in_specs=[pl.BlockSpec((rows, 512), full)] * 4
            + [
                pl.BlockSpec((256, CB), lambda i, c: (0, c[0] * NCB + i)),
                pl.BlockSpec((256, CB), lambda i, c: (0, i)),
            ],
            out_specs=pl.BlockSpec((rows, CB), lambda i, c: (0, i)),
            scratch_shapes=[pltpu.VMEM((rows, 256), bf16), pltpu.VMEM((rows, 256), bf16)],
        ),
        out_shape=jax.ShapeDtypeStruct((rows, HALF), bf16),
        compiler_params=pltpu.CompilerParams(vmem_limit_bytes=24 * MB),
        cost_estimate=pl.CostEstimate(flops=2 * rows * HALF * 512, bytes_accessed=11 * MB, transcendentals=rows * 512),
    )(core, own, own_add, sib, sib_add, wd, wr)


def total_kernel(c_ref, r_ref, sum_ref, send_ref):
    c = c_ref[0]
    r = r_ref[...].reshape(NEXP, 4, 2 * CAP, CB)
    total = r[:, 0].astype(f32) + r[:, 1].astype(f32) + (r[:, 2].astype(f32) + r[:, 3].astype(f32))
    total = total.reshape(NEXP * 2 * CAP, CB).astype(bf16)
    sum_ref[...] = total
    row = lax.broadcasted_iota(jnp.int32, (64, 128), 0)
    col = lax.broadcasted_iota(jnp.int32, (64, 128), 1)
    pick = jnp.where(col == (row // 4) * 8 + (1 - c) * 4 + row % 4, 1.0, 0.0).astype(bf16)
    send_ref[...] = jnp.dot(pick, total, preferred_element_type=f32).astype(bf16)


def total_rows(core, r):
    return pl.pallas_call(
        total_kernel,
        grid_spec=pltpu.PrefetchScalarGridSpec(
            num_scalar_prefetch=1,
            grid=(NCB,),
            in_specs=[pl.BlockSpec((4 * NEXP, 2 * CAP, CB), lambda i, c: (0, 0, i))],
            out_specs=[
                pl.BlockSpec((128, CB), lambda i, c: (0, i)),
                pl.BlockSpec((64, CB), lambda i, c: (0, i)),
            ],
        ),
        out_shape=[jax.ShapeDtypeStruct((128, HALF), bf16), jax.ShapeDtypeStruct((64, HALF), bf16)],
        compiler_params=pltpu.CompilerParams(vmem_limit_bytes=16 * MB),
        cost_estimate=pl.CostEstimate(flops=2 * 64 * 128 * HALF, bytes_accessed=6 * MB, transcendentals=0),
    )(core, r)


def place_kernel(c_ref, ids_ref, gates_ref, sum_ref, got_ref, out_ref, sel_own, sel_got):
    c = c_ref[0]

    @pl.when(jnp.logical_and(pl.program_id(0) == 0, pl.program_id(1) == 0))
    def _():
        own, _g = slot_select(ids_ref[...], None, c, True)
        sel_own[...] = own.astype(bf16)
        got, _h = slot_select(ids_ref[...], None, c, False)
        sel_got[...] = got.astype(bf16)

    gate = jnp.sum(jnp.where(ids_ref[...] < NEXP, gates_ref[...], 0.0), axis=1, keepdims=True)

    @pl.when(pl.program_id(0) == 0)
    def _():
        rows = jnp.dot(sel_own[...], sum_ref[...], preferred_element_type=f32)
        out_ref[...] = (rows * gate).astype(bf16)

    @pl.when(pl.program_id(0) == 1)
    def _():
        rows = jnp.dot(sel_got[...], got_ref[...], preferred_element_type=f32)
        out_ref[...] = (rows * gate).astype(bf16)


def place_rows(core, ids, gates, total, got):
    n = ids.shape[0]
    return pl.pallas_call(
        place_kernel,
        grid_spec=pltpu.PrefetchScalarGridSpec(
            num_scalar_prefetch=1,
            grid=(2, NCB),
            in_specs=[
                pl.BlockSpec((n, 8), lambda h, i, c: (0, 0)),
                pl.BlockSpec((n, 8), lambda h, i, c: (0, 0)),
                pl.BlockSpec((128, CB), lambda h, i, c: (0, jnp.where(h == 0, i, NCB - 1))),
                pl.BlockSpec((64, CB), lambda h, i, c: (0, jnp.where(h == 0, 0, i))),
            ],
            out_specs=pl.BlockSpec((n, CB), lambda h, i, c: (0, jnp.where(h == 0, c[0], 1 - c[0]) * NCB + i)),
            scratch_shapes=[pltpu.VMEM((n, 128), bf16), pltpu.VMEM((n, 64), bf16)],
        ),
        out_shape=jax.ShapeDtypeStruct((n, 2 * HALF), bf16),
        compiler_params=pltpu.CompilerParams(vmem_limit_bytes=16 * MB),
        cost_estimate=pl.CostEstimate(flops=2 * 128 * 128 * 2 * HALF, bytes_accessed=3 * MB, transcendentals=0),
    )(core, ids, gates, total, got)


GROUP = 8
PIECE = 256
KB = 512


def attend_kernel(p_ref, nope_ref, rope_ref, ku_ref, vu_ref, *rest):
    pieces = rest[:8]
    out_ref, keys, q_ref, acc_ref, sems = rest[8:]
    me = p_ref[0]

    def copies():
        found = []
        for p in range(8):
            for b in range(8):
                start = pl.multiple_of(p_ref[1 + p * 8 + b] * 64, 64)
                found.append(
                    pltpu.make_async_copy(pieces[p].at[b], keys.at[pl.ds(start, 64), :], sems.at[p * 8 + b])
                )
        return found

    first = pl.program_id(0) == 0

    @pl.when(first)
    def _():
        for copy in copies():
            copy.start()

    q_ref[:, LAT + ROPE :] = jnp.zeros((GROUP * 64, KW - LAT - ROPE), bf16)
    for h in range(GROUP):
        rows = pl.ds(h * 64, 64)
        q = lax.dot_general(
            nope_ref[:, h * NOPE : (h + 1) * NOPE], ku_ref[h], (((1,), (1,)), ((), ())), preferred_element_type=f32
        )
        q_ref[rows, :LAT] = q.astype(bf16)
        q_ref[rows, LAT : LAT + ROPE] = rope_ref[:, h * ROPE : (h + 1) * ROPE]

    @pl.when(first)
    def _():
        for copy in copies():
            copy.wait()

    scale = (NOPE + ROPE) ** -0.5 * 1.4426950408889634
    n_piece = GROUP * 64 // PIECE

    def chunk(j, stats, masked):
        k = keys[pl.ds(pl.multiple_of(j * KB, KB), KB), :]
        fresh = []
        for i in range(n_piece):
            m, l = stats[i]
            rows = pl.ds(i * PIECE, PIECE)
            s = lax.dot_general(q_ref[rows, :], k, (((1,), (1,)), ((), ())), preferred_element_type=f32)
            if masked:
                key_place = j * KB + lax.broadcasted_iota(jnp.int32, (PIECE, KB), 1)
                place = me * 64 + lax.broadcasted_iota(jnp.int32, (PIECE, KB), 0) % 64
                s = jnp.where(key_place <= place, s, -1e30)
            m_new = jnp.maximum(m, jnp.max(s, axis=1, keepdims=True))
            e = jnp.exp2(s * scale - m_new * scale)
            shrink = jnp.exp2((m - m_new) * scale)
            l_new = l * shrink + jnp.sum(e, axis=1, keepdims=True)
            pv = jnp.dot(e.astype(bf16), k[:, :LAT], preferred_element_type=f32)
            acc_ref[rows, :] = acc_ref[rows, :] * shrink + pv
            fresh.append((m_new, l_new))
        return tuple(fresh)

    acc_ref[...] = jnp.zeros_like(acc_ref)
    start = tuple(
        (jnp.full((PIECE, 1), -1e30, f32), jnp.zeros((PIECE, 1), f32)) for _ in range(n_piece)
    )
    last = me // (KB // 64)
    stats = chunk(last, start, True)
    stats = lax.fori_loop(0, last, lambda j, st: chunk(j, st, False), stats)
    for i in range(n_piece):
        rows = pl.ds(i * PIECE, PIECE)
        o = (acc_ref[rows, :] / stats[i][1]).astype(bf16)
        for h in range(PIECE // 64):
            head = i * (PIECE // 64) + h
            v = jnp.dot(o[h * 64 : (h + 1) * 64, :], vu_ref[head], preferred_element_type=f32)
            out_ref[:, head * 128 : (head + 1) * 128] = v.astype(bf16)


def attend(places, nope, rope, key_up, value_up, pieces):
    heads = key_up.shape[0]
    n = nope.shape[0]
    return pl.pallas_call(
        attend_kernel,
        grid_spec=pltpu.PrefetchScalarGridSpec(
            num_scalar_prefetch=1,
            grid=(heads // GROUP,),
            in_specs=[
                pl.BlockSpec((n, GROUP * NOPE), lambda i, p: (0, i)),
                pl.BlockSpec((n, GROUP * ROPE), lambda i, p: (0, i)),
                pl.BlockSpec((GROUP, LAT, NOPE), lambda i, p: (i, 0, 0)),
                pl.BlockSpec((GROUP, LAT, 128), lambda i, p: (i, 0, 0)),
            ]
            + [pl.BlockSpec(memory_space=pl.ANY)] * 8,
            out_specs=pl.BlockSpec((n, GROUP * 128), lambda i, p: (0, i)),
            scratch_shapes=[
                pltpu.VMEM((4096, KW), bf16),
                pltpu.VMEM((GROUP * 64, KW), bf16),
                pltpu.VMEM((GROUP * 64, LAT), f32),
                pltpu.SemaphoreType.DMA((64,)),
            ],
        ),
        out_shape=jax.ShapeDtypeStruct((n, heads * 128), bf16),
        compiler_params=pltpu.CompilerParams(vmem_limit_bytes=40 * MB),
        cost_estimate=pl.CostEstimate(
            flops=2 * 2048 * 4096 * 1152, bytes_accessed=12 * MB, transcendentals=2048 * 4096
        ),
    )(places, nope, rope, key_up, value_up, *pieces)


def ring(x, axis, step):
    return lax.ppermute(x, axis, [(i, (i + step) % 4) for i in range(4)])


def gather_keys(key_latent, key_rope):
    n = key_latent.shape[0]
    own = jnp.concatenate([key_latent, key_rope, jnp.zeros((n, KW - LAT - ROPE), bf16)], axis=1)
    z_axis = ("zh", "zl")
    by_z = jnp.stack([own] + [ring(own, z_axis, s) for s in (1, 2, 3)])
    by_x = jnp.concatenate([by_z, lax.ppermute(by_z, "xl", [(0, 1), (1, 0)])], axis=0)
    by_y = [by_x] + [ring(by_x, "y", s) for s in (1, 2, 3)]
    pieces = by_y + [swap_core(v) for v in by_y]
    xl, y, core = lax.axis_index("xl"), lax.axis_index("y"), lax.axis_index("core")
    z = lax.axis_index(z_axis)
    places = []
    for flip in (0, 1):
        for sy in range(4):
            for sx in (0, 1):
                for sz in range(4):
                    at = ((xl ^ sx) * 4 + (y - sy) % 4) * 4 + (z - sz) % 4
                    places.append(at * 2 + (core ^ flip))
    return pieces, places


def local(
    query_nope,
    query_rope,
    key_latent,
    key_rope,
    key_up,
    value_up,
    routed_tokens,
    expert_ids,
    expert_gates,
    gate_weight,
    up_weight,
    down_weight,
):
    c = lax.axis_index("core")
    core = c.reshape(1).astype(jnp.int32)
    other = (1 - c) * HALF
    tok_sib = swap_core(lax.dynamic_slice_in_dim(routed_tokens, other, HALF, 1))
    ids_sib = swap_core(expert_ids)
    outgoing = pack_rows(core, expert_ids, ids_sib, routed_tokens, tok_sib)
    arrived = lax.all_to_all(outgoing, CHIPS, split_axis=0, concat_axis=0, tiled=True)
    wg_sib = swap_core(lax.dynamic_slice_in_dim(gate_weight, other, HALF, 0))
    wu_sib = swap_core(lax.dynamic_slice_in_dim(up_weight, other, HALF, 0))
    wd_sib = swap_core(lax.dynamic_slice_in_dim(down_weight, other, HALF, 1))
    pieces, places = gather_keys(key_latent, key_rope)

    x = arrived.reshape(512, HALF)
    for_sib = gate_up(core, x, wg_sib, wu_sib)
    own_add = swap_core(for_sib)
    own = gate_up(core, x, gate_weight, up_weight)
    sib_add = swap_core(own)
    y = down(core, own, own_add, for_sib, sib_add, down_weight, wd_sib)
    y, pieces = lax.optimization_barrier((y, pieces))
    returned = lax.all_to_all(y.reshape(64, 8, HALF), CHIPS, split_axis=0, concat_axis=0, tiled=True)

    me = lax.axis_index(CTX)
    table = jnp.stack([me] + places).astype(jnp.int32)
    attention_out = attend(table, query_nope, query_rope, key_up, value_up, pieces)

    total, send = total_rows(core, returned)
    got = swap_core(send)
    routed_out = place_rows(core, expert_ids, expert_gates, total, got)
    return attention_out, routed_out


def solution(mesh):
    fine = Mesh(mesh.devices.reshape(2, 4, 2, 2, 2, 2), AXES)
    every = P(AXES)
    return jax.shard_map(
        local,
        mesh=fine,
        in_specs=(
            P(CTX, "sec"),
            P(CTX, "sec"),
            P(CTX, None),
            P(CTX, None),
            P("sec", None, None),
            P("sec", None, None),
            every,
            every,
            every,
            P(None, AXES),
            P(None, AXES),
            every,
        ),
        out_specs=(P(CTX, "sec"), every),
        check_vma=False,
    )
```

```python
import functools

import jax
import jax.numpy as jnp
from jax import lax
from jax.experimental import pallas as pl
from jax.experimental.pallas import tpu as pltpu
from jax.sharding import Mesh
from jax.sharding import PartitionSpec as P

AXES = ("xl", "y", "zh", "zl", "core", "sec")
CTX = ("xl", "y", "zh", "zl", "core")
CHIPS = ("xl", "y", "zh", "zl", "sec")
ROPE = 64
NOPE = 128
LAT = 512
KW = 640
CAP = 4
EB = 4
NEB = 4
SLOTS = 128
NEXP = 16
HALF = 3584
CB = 512
NCB = HALF // CB
WB = 512
NWB = HALF // WB
MB = 1024 * 1024
SMALL = 24 * MB
LARGE = 56 * MB
bf16 = jnp.bfloat16
f32 = jnp.float32


def swap_core(x):
    return lax.ppermute(x, "core", [(0, 1), (1, 0)])


def slot_select(ids, side):
    tokens = ids.shape[0]
    col = lax.broadcasted_iota(jnp.int32, (tokens, SLOTS), 1)
    named = jnp.zeros((tokens, SLOTS), f32)
    for k in range(ids.shape[1]):
        named = named + jnp.where(ids[:, k : k + 1] == col // 8, 1.0, 0.0)
    row_i = lax.broadcasted_iota(jnp.int32, (tokens, tokens), 0)
    col_i = lax.broadcasted_iota(jnp.int32, (tokens, tokens), 1)
    before = jnp.where(col_i < row_i, 1.0, 0.0).astype(bf16)
    rank = jnp.dot(before, named.astype(bf16), preferred_element_type=f32)
    hit = jnp.logical_and(named > 0.5, rank == (col % 4).astype(f32))
    hit = jnp.logical_and(hit, (col // 4) % 2 == side)
    return jnp.where(hit, 1.0, 0.0)


def select_kernel(ids_ref, pack_lo, pack_hi, place_lo, place_hi):
    for side, pack, place in ((0, pack_lo, place_lo), (1, pack_hi, place_hi)):
        chosen = slot_select(ids_ref[...], side)
        pack[...] = chosen.T.astype(bf16)
        place[...] = chosen.astype(bf16)


def select(ids):
    n = ids.shape[0]
    shapes = [(SLOTS, n), (SLOTS, n), (n, SLOTS), (n, SLOTS)]
    return pl.pallas_call(
        select_kernel,
        out_shape=[jax.ShapeDtypeStruct(shape, bf16) for shape in shapes],
        compiler_params=pltpu.CompilerParams(vmem_limit_bytes=SMALL),
        cost_estimate=pl.CostEstimate(flops=4 * MB, bytes_accessed=MB // 4, transcendentals=0),
    )(ids)


def pack_kernel(sel_lo, sel_hi, tok_lo, tok_hi, out_ref):
    rows = jnp.dot(sel_lo[...], tok_lo[...], preferred_element_type=f32)
    rows = rows + jnp.dot(sel_hi[...], tok_hi[...], preferred_element_type=f32)
    rows = rows.astype(bf16).reshape(NEXP, 1, 2 * CAP, CB)
    out_ref[...] = jnp.broadcast_to(rows, (NEXP, 4, 2 * CAP, CB)).reshape(4 * NEXP, 2 * CAP, CB)


def pack_rows(sel_lo, sel_hi, tokens):
    n = tokens.shape[0]
    return pl.pallas_call(
        pack_kernel,
        grid=(NCB,),
        in_specs=[
            pl.BlockSpec((SLOTS, n), lambda i: (0, 0)),
            pl.BlockSpec((SLOTS, n), lambda i: (0, 0)),
            pl.BlockSpec((n, CB), lambda i: (0, i)),
            pl.BlockSpec((n, CB), lambda i: (0, NCB + i)),
        ],
        out_specs=pl.BlockSpec((4 * NEXP, 2 * CAP, CB), lambda i: (0, 0, i)),
        out_shape=jax.ShapeDtypeStruct((4 * NEXP, 2 * CAP, HALF), bf16),
        compiler_params=pltpu.CompilerParams(vmem_limit_bytes=SMALL),
        cost_estimate=pl.CostEstimate(flops=2 * 128 * 256 * HALF, bytes_accessed=6 * MB, transcendentals=0),
    )(sel_lo, sel_hi, tokens, tokens)


def expert_kernel(x_ref, *rest):
    weights = rest[:8]
    downs = rest[8:12]
    out_ref, acc, hidden = rest[12:]
    step = pl.program_id(0)
    low = lax.broadcasted_iota(jnp.int32, (32, 8, WB), 1) < CAP

    def part(pair, fill):
        return jnp.where(low, pair, fill)

    @pl.when(step < NWB)
    def _():
        x = x_ref[...].astype(f32).reshape(32, 2, 8, WB)
        even, odd = x[:, 0], x[:, 1]
        x_lo = part(even, pltpu.roll(odd, CAP, 1)).reshape(256, WB).astype(bf16)
        x_hi = part(pltpu.roll(even, CAP, 1), odd).reshape(256, WB).astype(bf16)
        for i in range(4):
            cols = slice(i * 256, (i + 1) * 256)
            g = jnp.dot(x_lo, weights[2 * i][...], preferred_element_type=f32)
            g = g + jnp.dot(x_hi, weights[2 * i + 1][...], preferred_element_type=f32)
            acc[:, cols] = jnp.where(step == 0, g, acc[:, cols] + g)

    @pl.when(step == NWB - 1)
    def _():
        g, u = acc[:, :512], acc[:, 512:]
        hidden[...] = (g / (1.0 + jnp.exp(-g)) * u).astype(bf16)

    @pl.when(step >= NWB)
    def _():
        h_own, h_sib = hidden[:, :256], hidden[:, 256:]
        y = []
        for i in range(2):
            v = jnp.dot(h_own, downs[i][...], preferred_element_type=f32)
            v = v + jnp.dot(h_sib, downs[2 + i][...], preferred_element_type=f32)
            y.append(v.reshape(32, 8, WB))
        even = part(y[0], pltpu.roll(y[1], CAP, 1))
        odd = part(pltpu.roll(y[0], CAP, 1), y[1])
        out = jnp.concatenate([even[:, None], odd[:, None]], axis=1)
        out_ref[...] = out.reshape(64, 8, WB).astype(bf16)


def experts(x, gate, gate_sib, up, up_sib, wd, wd_sib):
    k = lambda i: jnp.minimum(i, NWB - 1)
    n = lambda i: jnp.maximum(i - NWB, 0)
    first = [pl.BlockSpec((WB, 256), lambda i: (k(i), 0)), pl.BlockSpec((WB, 256), lambda i: (NWB + k(i), 0))]
    second = [pl.BlockSpec((256, WB), lambda i: (0, n(i))), pl.BlockSpec((256, WB), lambda i: (0, NWB + n(i)))]
    return pl.pallas_call(
        expert_kernel,
        grid=(2 * NWB,),
        in_specs=[pl.BlockSpec((64, 8, WB), lambda i: (0, 0, k(i)))] + first * 4 + second * 2,
        out_specs=pl.BlockSpec((64, 8, WB), lambda i: (0, 0, n(i))),
        out_shape=jax.ShapeDtypeStruct((64, 8, HALF), bf16),
        scratch_shapes=[pltpu.VMEM((256, 1024), f32), pltpu.VMEM((256, 512), bf16)],
        compiler_params=pltpu.CompilerParams(vmem_limit_bytes=LARGE),
        cost_estimate=pl.CostEstimate(
            flops=2 * 256 * 7168 * 1536, bytes_accessed=30 * MB, transcendentals=256 * 512
        ),
    )(x, gate, gate, gate_sib, gate_sib, up, up, up_sib, up_sib, wd, wd, wd_sib, wd_sib)


def place_kernel(r_ref, sel_lo, sel_hi, gate_ref, out_ref, total):
    step = pl.program_id(0)

    @pl.when(step < NEB)
    def _():
        r = r_ref[...].reshape(EB, 4, 2 * CAP, HALF)
        rows = r[:, 0].astype(f32) + r[:, 1].astype(f32) + (r[:, 2].astype(f32) + r[:, 3].astype(f32))
        start = pl.multiple_of(step * EB * 2 * CAP, EB * 2 * CAP)
        total[pl.ds(start, EB * 2 * CAP), :] = rows.reshape(EB * 2 * CAP, HALF).astype(bf16)

    for side, sel in ((0, sel_lo), (1, sel_hi)):

        @pl.when(step == NEB + side)
        def _():
            rows = jnp.dot(sel[...], total[...], preferred_element_type=f32)
            out_ref[...] = (rows * gate_ref[...]).astype(bf16)


def place_rows(r, sel_lo, sel_hi, gate):
    n = gate.shape[0]
    full = lambda i: (0, 0)
    return pl.pallas_call(
        place_kernel,
        grid=(NEB + 2,),
        in_specs=[
            pl.BlockSpec((4 * EB, 2 * CAP, HALF), lambda i: (jnp.minimum(i, NEB - 1), 0, 0)),
            pl.BlockSpec((n, SLOTS), full),
            pl.BlockSpec((n, SLOTS), full),
            pl.BlockSpec((n, 1), full),
        ],
        out_specs=pl.BlockSpec((n, HALF), lambda i: (0, jnp.maximum(i - NEB, 0))),
        out_shape=jax.ShapeDtypeStruct((n, 2 * HALF), bf16),
        scratch_shapes=[pltpu.VMEM((SLOTS, HALF), bf16)],
        compiler_params=pltpu.CompilerParams(vmem_limit_bytes=SMALL),
        cost_estimate=pl.CostEstimate(flops=2 * 128 * 128 * 2 * HALF, bytes_accessed=6 * MB, transcendentals=0),
    )(r, sel_lo, sel_hi, gate)


GROUP = 16
PIECE = 256
KB = 1024


def attend_kernel(p_ref, nope_ref, rope_ref, ku_ref, vu_ref, *rest):
    pieces = rest[:8]
    out_ref, keys, q_ref, acc_ref, sems = rest[8:]
    me = p_ref[0]

    def copies():
        found = []
        for piece in pieces:
            for b in range(piece.shape[0]):
                n = len(found)
                start = pl.multiple_of(p_ref[1 + n] * 64, 64)
                found.append(pltpu.make_async_copy(piece.at[b], keys.at[pl.ds(start, 64), :], sems.at[n]))
        return found

    first = pl.program_id(0) == 0

    @pl.when(first)
    def _():
        for copy in copies():
            copy.start()

    q_ref[:, LAT + ROPE :] = jnp.zeros((GROUP * 64, KW - LAT - ROPE), bf16)
    for h in range(GROUP):
        rows = pl.ds(h * 64, 64)
        q = lax.dot_general(
            nope_ref[:, h * NOPE : (h + 1) * NOPE], ku_ref[h], (((1,), (1,)), ((), ())), preferred_element_type=f32
        )
        q_ref[rows, :LAT] = q.astype(bf16)
        q_ref[rows, LAT : LAT + ROPE] = rope_ref[:, h * ROPE : (h + 1) * ROPE]

    @pl.when(first)
    def _():
        for copy in copies():
            copy.wait()

    scale = (NOPE + ROPE) ** -0.5 * 1.4426950408889634
    n_piece = GROUP * 64 // PIECE

    def score(j, i, masked):
        k = keys[pl.ds(pl.multiple_of(j * KB, KB), KB), :]
        q = q_ref[pl.ds(i * PIECE, PIECE), :]
        s = lax.dot_general(q, k, (((1,), (1,)), ((), ())), preferred_element_type=f32)
        if masked:
            key_place = j * KB + lax.broadcasted_iota(jnp.int32, (PIECE, KB), 1)
            place = me * 64 + lax.broadcasted_iota(jnp.int32, (PIECE, KB), 0) % 64
            s = jnp.where(key_place <= place, s, -1e30)
        return s

    def update(j, i, s, stat):
        m, l = stat
        rows = pl.ds(i * PIECE, PIECE)
        values = keys[pl.ds(pl.multiple_of(j * KB, KB), KB), :LAT]
        m_new = jnp.maximum(m, jnp.max(s, axis=1, keepdims=True))
        e = jnp.exp2(s * scale - m_new * scale)
        shrink = jnp.exp2((m - m_new) * scale)
        part = e[:, :128]
        for t in range(1, KB // 128):
            part = part + e[:, t * 128 : (t + 1) * 128]
        pv = jnp.dot(e.astype(bf16), values, preferred_element_type=f32)
        acc_ref[rows, :] = acc_ref[rows, :] * shrink + pv
        return m_new, l * shrink + part

    def chunk(j, stats, masked):
        s = score(j, 0, masked)
        fresh = []
        for i in range(n_piece):
            ahead = score(j, i + 1, masked) if i + 1 < n_piece else None
            fresh.append(update(j, i, s, stats[i]))
            s = ahead
        return tuple(fresh)

    acc_ref[...] = jnp.zeros_like(acc_ref)
    start = tuple(
        (jnp.full((PIECE, 1), -1e30, f32), jnp.zeros((PIECE, 128), f32)) for _ in range(n_piece)
    )
    last = me // (KB // 64)
    stats = chunk(last, start, True)
    stats = lax.fori_loop(0, last, lambda j, st: chunk(j, st, False), stats)
    for i in range(n_piece):
        rows = pl.ds(i * PIECE, PIECE)
        o = (acc_ref[rows, :] / jnp.sum(stats[i][1], axis=1, keepdims=True)).astype(bf16)
        for h in range(PIECE // 64):
            head = i * (PIECE // 64) + h
            v = jnp.dot(o[h * 64 : (h + 1) * 64, :], vu_ref[head], preferred_element_type=f32)
            out_ref[:, head * 128 : (head + 1) * 128] = v.astype(bf16)


def attend(places, nope, rope, key_up, value_up, pieces):
    heads = key_up.shape[0]
    n = nope.shape[0]
    return pl.pallas_call(
        attend_kernel,
        grid_spec=pltpu.PrefetchScalarGridSpec(
            num_scalar_prefetch=1,
            grid=(heads // GROUP,),
            in_specs=[
                pl.BlockSpec((n, GROUP * NOPE), lambda i, p: (0, i)),
                pl.BlockSpec((n, GROUP * ROPE), lambda i, p: (0, i)),
                pl.BlockSpec((GROUP, LAT, NOPE), lambda i, p: (i, 0, 0)),
                pl.BlockSpec((GROUP, LAT, 128), lambda i, p: (i, 0, 0)),
            ]
            + [pl.BlockSpec(memory_space=pl.ANY)] * 8,
            out_specs=pl.BlockSpec((n, GROUP * 128), lambda i, p: (0, i)),
            scratch_shapes=[
                pltpu.VMEM((4096, KW), bf16),
                pltpu.VMEM((GROUP * 64, KW), bf16),
                pltpu.VMEM((GROUP * 64, LAT), f32),
                pltpu.SemaphoreType.DMA((64,)),
            ],
        ),
        out_shape=jax.ShapeDtypeStruct((n, heads * 128), bf16),
        compiler_params=pltpu.CompilerParams(vmem_limit_bytes=LARGE),
        cost_estimate=pl.CostEstimate(
            flops=2 * 2048 * 4096 * 1152, bytes_accessed=12 * MB, transcendentals=2048 * 4096
        ),
    )(places, nope, rope, key_up, value_up, *pieces)


def ring(x, axis, step):
    return lax.ppermute(x, axis, [(i, (i + step) % 4) for i in range(4)])


Z_AXIS = ("zh", "zl")


def plane_keys(key_latent, key_rope, outgoing):
    n = key_latent.shape[0]
    own = jnp.concatenate([key_latent, key_rope, jnp.zeros((n, KW - LAT - ROPE), bf16)], axis=1)
    by_z = jnp.stack([own] + [ring(own, Z_AXIS, s) for s in (1, 2, 3)])
    outgoing, by_z = lax.optimization_barrier((outgoing, by_z))
    return outgoing, [by_z] + [ring(by_z, "y", s) for s in (1, 2, 3)]


def first_half(plane):
    near = lax.ppermute(plane[0], ("xl", "sec"), [(0, 2), (1, 3)])
    far = lax.ppermute(plane[1], ("xl", "sec"), [(0, 3), (1, 2)])
    return [near, far]


def key_places():
    xl, y, core = lax.axis_index("xl"), lax.axis_index("y"), lax.axis_index("core")
    z = lax.axis_index(Z_AXIS)
    i = jnp.arange(64, dtype=jnp.int32)
    flip, early, sy, sz = i // 32, (i // 16) % 2, (i // 4) % 4, i % 4
    half = jnp.where(early == 1, 1 - xl, xl)
    at = (half * 4 + ((y - sy) & 3)) * 4 + ((z - sz) & 3)
    return at * 2 + (core ^ flip)


def local(
    query_nope,
    query_rope,
    key_latent,
    key_rope,
    key_up,
    value_up,
    routed_tokens,
    expert_ids,
    expert_gates,
    gate_weight,
    up_weight,
    down_weight,
):
    pack_lo, pack_hi, place_lo, place_hi = select(expert_ids)
    outgoing = pack_rows(pack_lo, pack_hi, routed_tokens)
    outgoing, plane = plane_keys(key_latent, key_rope, outgoing)
    arrived = lax.all_to_all(outgoing, CHIPS, split_axis=0, concat_axis=0, tiled=True)
    gate = jnp.sum(jnp.where(expert_ids < NEXP, expert_gates, 0.0), axis=1, keepdims=True)
    gate_sib, up_sib = swap_core(gate_weight), swap_core(up_weight)
    wd_sib = swap_core(lax.optimization_barrier((down_weight, gate_sib))[0])
    arrived, plane = lax.optimization_barrier((arrived, plane))
    plane = [jnp.concatenate(plane[:2], axis=0), jnp.concatenate(plane[2:], axis=0)]
    early = first_half(plane)
    plane_sib = [swap_core(v) for v in plane]

    y = experts(arrived, gate_weight, gate_sib, up_weight, up_sib, down_weight, wd_sib)
    y, early, plane_sib = lax.optimization_barrier((y, early, plane_sib))
    pieces = plane + early + plane_sib + [swap_core(v) for v in early]
    pieces = lax.optimization_barrier((pieces, y))[0]
    returned = lax.all_to_all(y, CHIPS, split_axis=0, concat_axis=0, tiled=True)

    me = lax.axis_index(CTX).reshape(1).astype(jnp.int32)
    table = jnp.concatenate([me, key_places()])
    attention_out = attend(table, query_nope, query_rope, key_up, value_up, pieces)
    returned, attention_out = lax.optimization_barrier((returned, attention_out))

    routed_out = place_rows(returned, place_lo, place_hi, gate)
    return attention_out, routed_out


def solution(mesh):
    fine = Mesh(mesh.devices.reshape(2, 4, 2, 2, 2, 2), AXES)
    every = P(AXES)
    return jax.shard_map(
        local,
        mesh=fine,
        in_specs=(
            P(CTX, "sec"),
            P(CTX, "sec"),
            P(CTX, None),
            P(CTX, None),
            P("sec", None, None),
            P("sec", None, None),
            every,
            every,
            every,
            P(None, AXES),
            P(None, AXES),
            every,
        ),
        out_specs=(P(CTX, "sec"), every),
        check_vma=False,
    )
```

```python
import functools

import jax
import jax.numpy as jnp
from jax import lax
from jax.experimental import pallas as pl
from jax.experimental.pallas import tpu as pltpu
from jax.sharding import Mesh
from jax.sharding import PartitionSpec as P

AXES = ("xl", "y", "zh", "zl", "core", "sec")
CTX = ("xl", "y", "zh", "zl", "core")
CHIPS = ("xl", "y", "zh", "zl", "sec")
ROPE = 64
NOPE = 128
LAT = 512
KW = 640
CAP = 4
EB = 4
NEB = 4
SLOTS = 128
NEXP = 16
HALF = 3584
CB = 1792
NCB = HALF // CB
WB = 1792
NWB = HALF // WB
MB = 1024 * 1024
SMALL = 24 * MB
LARGE = 56 * MB
bf16 = jnp.bfloat16
f32 = jnp.float32


def swap_core(x):
    return lax.ppermute(x, "core", [(0, 1), (1, 0)])


def slot_select(ids, side):
    tokens = ids.shape[1]
    slot = lax.broadcasted_iota(jnp.int32, (SLOTS, tokens), 0)
    named = jnp.zeros((SLOTS, tokens), f32)
    for k in range(ids.shape[0]):
        named = named + jnp.where(ids[k : k + 1, :] == slot // 8, 1.0, 0.0)
    row_i = lax.broadcasted_iota(jnp.int32, (tokens, tokens), 0)
    col_i = lax.broadcasted_iota(jnp.int32, (tokens, tokens), 1)
    before = jnp.where(row_i < col_i, 1.0, 0.0).astype(bf16)
    rank = jnp.dot(named.astype(bf16), before, preferred_element_type=f32)
    hit = jnp.logical_and(named > 0.5, rank == (slot % 4).astype(f32))
    hit = jnp.logical_and(hit, (slot // 4) % 2 == side)
    return jnp.where(hit, 1.0, 0.0)


def pack_kernel(ids_ref, tok_lo, tok_hi, out_ref, place_lo, place_hi, sel_lo, sel_hi):
    @pl.when(pl.program_id(0) == 0)
    def _():
        for side, sel, place in ((0, sel_lo, place_lo), (1, sel_hi, place_hi)):
            chosen = slot_select(ids_ref[...], side)
            sel[...] = chosen.astype(bf16)
            place[...] = chosen.T.astype(bf16)

    rows = jnp.dot(sel_lo[...], tok_lo[...], preferred_element_type=f32)
    rows = rows + jnp.dot(sel_hi[...], tok_hi[...], preferred_element_type=f32)
    rows = rows.astype(bf16).reshape(NEXP, 1, 2 * CAP, CB)
    out_ref[...] = jnp.broadcast_to(rows, (NEXP, 4, 2 * CAP, CB)).reshape(4 * NEXP, 2 * CAP, CB)


def pack_rows(ids, tokens):
    n = tokens.shape[0]
    return pl.pallas_call(
        pack_kernel,
        grid=(NCB,),
        in_specs=[
            pl.BlockSpec((8, n), lambda i: (0, 0)),
            pl.BlockSpec((n, CB), lambda i: (0, i)),
            pl.BlockSpec((n, CB), lambda i: (0, NCB + i)),
        ],
        out_specs=[
            pl.BlockSpec((4 * NEXP, 2 * CAP, CB), lambda i: (0, 0, i)),
            pl.BlockSpec((n, SLOTS), lambda i: (0, 0)),
            pl.BlockSpec((n, SLOTS), lambda i: (0, 0)),
        ],
        out_shape=[
            jax.ShapeDtypeStruct((4 * NEXP, 2 * CAP, HALF), bf16),
            jax.ShapeDtypeStruct((n, SLOTS), bf16),
            jax.ShapeDtypeStruct((n, SLOTS), bf16),
        ],
        scratch_shapes=[pltpu.VMEM((SLOTS, n), bf16), pltpu.VMEM((SLOTS, n), bf16)],
        compiler_params=pltpu.CompilerParams(vmem_limit_bytes=LARGE),
        cost_estimate=pl.CostEstimate(flops=2 * 128 * 256 * HALF, bytes_accessed=6 * MB, transcendentals=0),
    )(ids, tokens, tokens)


def expert_kernel(x_ref, *rest):
    weights = rest[:8]
    downs = rest[8:12]
    out_ref, acc, hidden = rest[12:]
    step = pl.program_id(0)
    low = lax.broadcasted_iota(jnp.int32, (32, 8, WB), 1) < CAP

    def part(pair, fill):
        return jnp.where(low, pair, fill)

    @pl.when(step < NWB)
    def _():
        x = x_ref[...].astype(f32).reshape(32, 2, 8, WB)
        even, odd = x[:, 0], x[:, 1]
        x_lo = part(even, pltpu.roll(odd, CAP, 1)).reshape(256, WB).astype(bf16)
        x_hi = part(pltpu.roll(even, CAP, 1), odd).reshape(256, WB).astype(bf16)
        for i in range(4):
            cols = slice(i * 256, (i + 1) * 256)
            g = jnp.dot(x_lo, weights[2 * i][...], preferred_element_type=f32)
            g = g + jnp.dot(x_hi, weights[2 * i + 1][...], preferred_element_type=f32)
            acc[:, cols] = jnp.where(step == 0, g, acc[:, cols] + g)

    @pl.when(step == NWB - 1)
    def _():
        g, u = acc[:, :512], acc[:, 512:]
        hidden[...] = (g / (1.0 + jnp.exp(-g)) * u).astype(bf16)

    @pl.when(step >= NWB)
    def _():
        h_own, h_sib = hidden[:, :256], hidden[:, 256:]
        y = []
        for i in range(2):
            v = jnp.dot(h_own, downs[i][...], preferred_element_type=f32)
            v = v + jnp.dot(h_sib, downs[2 + i][...], preferred_element_type=f32)
            y.append(v.reshape(32, 8, WB))
        even = part(y[0], pltpu.roll(y[1], CAP, 1))
        odd = part(pltpu.roll(y[0], CAP, 1), y[1])
        out = jnp.concatenate([even[:, None], odd[:, None]], axis=1)
        out_ref[...] = out.reshape(64, 8, WB).astype(bf16)


def experts(x, gate, gate_sib, up, up_sib, wd, wd_sib):
    k = lambda i: jnp.minimum(i, NWB - 1)
    n = lambda i: jnp.maximum(i - NWB, 0)
    first = [pl.BlockSpec((WB, 256), lambda i: (k(i), 0)), pl.BlockSpec((WB, 256), lambda i: (NWB + k(i), 0))]
    second = [pl.BlockSpec((256, WB), lambda i: (0, n(i))), pl.BlockSpec((256, WB), lambda i: (0, NWB + n(i)))]
    return pl.pallas_call(
        expert_kernel,
        grid=(2 * NWB,),
        in_specs=[pl.BlockSpec((64, 8, WB), lambda i: (0, 0, k(i)))] + first * 4 + second * 2,
        out_specs=pl.BlockSpec((64, 8, WB), lambda i: (0, 0, n(i))),
        out_shape=jax.ShapeDtypeStruct((64, 8, HALF), bf16),
        scratch_shapes=[pltpu.VMEM((256, 1024), f32), pltpu.VMEM((256, 512), bf16)],
        compiler_params=pltpu.CompilerParams(vmem_limit_bytes=LARGE),
        cost_estimate=pl.CostEstimate(
            flops=2 * 256 * 7168 * 1536, bytes_accessed=30 * MB, transcendentals=256 * 512
        ),
    )(x, gate, gate, gate_sib, gate_sib, up, up, up_sib, up_sib, wd, wd, wd_sib, wd_sib)


def place_kernel(r_ref, sel_lo, sel_hi, gate_ref, out_ref, total):
    step = pl.program_id(0)

    @pl.when(step < NEB)
    def _():
        r = r_ref[...].reshape(EB, 4, 2 * CAP, HALF)
        rows = r[:, 0].astype(f32) + r[:, 1].astype(f32) + (r[:, 2].astype(f32) + r[:, 3].astype(f32))
        start = pl.multiple_of(step * EB * 2 * CAP, EB * 2 * CAP)
        total[pl.ds(start, EB * 2 * CAP), :] = rows.reshape(EB * 2 * CAP, HALF).astype(bf16)

    for side, sel in ((0, sel_lo), (1, sel_hi)):

        @pl.when(step == NEB + side)
        def _():
            rows = jnp.dot(sel[...], total[...], preferred_element_type=f32)
            out_ref[...] = (rows * gate_ref[...]).astype(bf16)


def place_rows(r, sel_lo, sel_hi, gate):
    n = gate.shape[0]
    full = lambda i: (0, 0)
    return pl.pallas_call(
        place_kernel,
        grid=(NEB + 2,),
        in_specs=[
            pl.BlockSpec((4 * EB, 2 * CAP, HALF), lambda i: (jnp.minimum(i, NEB - 1), 0, 0)),
            pl.BlockSpec((n, SLOTS), full),
            pl.BlockSpec((n, SLOTS), full),
            pl.BlockSpec((n, 1), full),
        ],
        out_specs=pl.BlockSpec((n, HALF), lambda i: (0, jnp.maximum(i - NEB, 0))),
        out_shape=jax.ShapeDtypeStruct((n, 2 * HALF), bf16),
        scratch_shapes=[pltpu.VMEM((SLOTS, HALF), bf16)],
        compiler_params=pltpu.CompilerParams(vmem_limit_bytes=SMALL),
        cost_estimate=pl.CostEstimate(flops=2 * 128 * 128 * 2 * HALF, bytes_accessed=6 * MB, transcendentals=0),
    )(r, sel_lo, sel_hi, gate)


GROUP = 16
PIECE = 256
KB = 1024


def attend_kernel(p_ref, nope_ref, rope_ref, ku_ref, vu_ref, *rest):
    pieces = rest[:8]
    out_ref, keys, q_ref, acc_ref, sems = rest[8:]
    me = p_ref[0]

    def copies():
        found = []
        for piece in pieces:
            for b in range(piece.shape[0]):
                n = len(found)
                start = pl.multiple_of(p_ref[1 + n] * 64, 64)
                found.append(pltpu.make_async_copy(piece.at[b], keys.at[pl.ds(start, 64), :], sems.at[n]))
        return found

    first = pl.program_id(0) == 0

    @pl.when(first)
    def _():
        for copy in copies():
            copy.start()

    q_ref[:, LAT + ROPE :] = jnp.zeros((GROUP * 64, KW - LAT - ROPE), bf16)
    for h in range(GROUP):
        rows = pl.ds(h * 64, 64)
        q = lax.dot_general(
            nope_ref[:, h * NOPE : (h + 1) * NOPE], ku_ref[h], (((1,), (1,)), ((), ())), preferred_element_type=f32
        )
        q_ref[rows, :LAT] = q.astype(bf16)
        q_ref[rows, LAT : LAT + ROPE] = rope_ref[:, h * ROPE : (h + 1) * ROPE]

    @pl.when(first)
    def _():
        for copy in copies():
            copy.wait()

    scale = (NOPE + ROPE) ** -0.5 * 1.4426950408889634
    n_piece = GROUP * 64 // PIECE

    def score(j, i, masked):
        k = keys[pl.ds(pl.multiple_of(j * KB, KB), KB), :]
        q = q_ref[pl.ds(i * PIECE, PIECE), :]
        s = lax.dot_general(q, k, (((1,), (1,)), ((), ())), preferred_element_type=f32)
        if masked:
            key_place = j * KB + lax.broadcasted_iota(jnp.int32, (PIECE, KB), 1)
            place = me * 64 + lax.broadcasted_iota(jnp.int32, (PIECE, KB), 0) % 64
            s = jnp.where(key_place <= place, s, -1e30)
        return s

    def update(j, i, s, stat):
        m, l = stat
        rows = pl.ds(i * PIECE, PIECE)
        values = keys[pl.ds(pl.multiple_of(j * KB, KB), KB), :LAT]
        m_new = jnp.maximum(m, jnp.max(s, axis=1, keepdims=True))
        e = jnp.exp2(s * scale - m_new * scale)
        shrink = jnp.exp2((m - m_new) * scale)
        part = e[:, :128]
        for t in range(1, KB // 128):
            part = part + e[:, t * 128 : (t + 1) * 128]
        pv = jnp.dot(e.astype(bf16), values, preferred_element_type=f32)
        acc_ref[rows, :] = acc_ref[rows, :] * shrink + pv
        return m_new, l * shrink + part

    def chunk(j, stats, masked):
        s = score(j, 0, masked)
        fresh = []
        for i in range(n_piece):
            ahead = score(j, i + 1, masked) if i + 1 < n_piece else None
            fresh.append(update(j, i, s, stats[i]))
            s = ahead
        return tuple(fresh)

    acc_ref[...] = jnp.zeros_like(acc_ref)
    start = tuple(
        (jnp.full((PIECE, 1), -1e30, f32), jnp.zeros((PIECE, 128), f32)) for _ in range(n_piece)
    )
    last = me // (KB // 64)
    stats = chunk(last, start, True)
    stats = lax.fori_loop(0, last, lambda j, st: chunk(j, st, False), stats)
    for i in range(n_piece):
        rows = pl.ds(i * PIECE, PIECE)
        o = (acc_ref[rows, :] / jnp.sum(stats[i][1], axis=1, keepdims=True)).astype(bf16)
        for h in range(PIECE // 64):
            head = i * (PIECE // 64) + h
            v = jnp.dot(o[h * 64 : (h + 1) * 64, :], vu_ref[head], preferred_element_type=f32)
            out_ref[:, head * 128 : (head + 1) * 128] = v.astype(bf16)


def attend(places, nope, rope, key_up, value_up, pieces):
    heads = key_up.shape[0]
    n = nope.shape[0]
    return pl.pallas_call(
        attend_kernel,
        grid_spec=pltpu.PrefetchScalarGridSpec(
            num_scalar_prefetch=1,
            grid=(heads // GROUP,),
            in_specs=[
                pl.BlockSpec((n, GROUP * NOPE), lambda i, p: (0, i)),
                pl.BlockSpec((n, GROUP * ROPE), lambda i, p: (0, i)),
                pl.BlockSpec((GROUP, LAT, NOPE), lambda i, p: (i, 0, 0)),
                pl.BlockSpec((GROUP, LAT, 128), lambda i, p: (i, 0, 0)),
            ]
            + [pl.BlockSpec(memory_space=pl.ANY)] * 8,
            out_specs=pl.BlockSpec((n, GROUP * 128), lambda i, p: (0, i)),
            scratch_shapes=[
                pltpu.VMEM((4096, KW), bf16),
                pltpu.VMEM((GROUP * 64, KW), bf16),
                pltpu.VMEM((GROUP * 64, LAT), f32),
                pltpu.SemaphoreType.DMA((64,)),
            ],
        ),
        out_shape=jax.ShapeDtypeStruct((n, heads * 128), bf16),
        compiler_params=pltpu.CompilerParams(vmem_limit_bytes=LARGE),
        cost_estimate=pl.CostEstimate(
            flops=2 * 2048 * 4096 * 1152, bytes_accessed=12 * MB, transcendentals=2048 * 4096
        ),
    )(places, nope, rope, key_up, value_up, *pieces)


def ring(x, axis, step):
    return lax.ppermute(x, axis, [(i, (i + step) % 4) for i in range(4)])


Z_AXIS = ("zh", "zl")


def plane_keys(key_latent, key_rope, outgoing):
    n = key_latent.shape[0]
    own = jnp.concatenate([key_latent, key_rope, jnp.zeros((n, KW - LAT - ROPE), bf16)], axis=1)
    by_z = jnp.stack([own] + [ring(own, Z_AXIS, s) for s in (1, 2, 3)])
    outgoing, by_z = lax.optimization_barrier((outgoing, by_z))
    return outgoing, [by_z] + [ring(by_z, "y", s) for s in (1, 2, 3)]


def to_second_half(keys, far=False):
    return lax.ppermute(keys, ("xl", "sec"), [(0, 3), (1, 2)] if far else [(0, 2), (1, 3)])


def key_places():
    xl, y, core = lax.axis_index("xl"), lax.axis_index("y"), lax.axis_index("core")
    z = lax.axis_index(Z_AXIS)
    i = jnp.arange(64, dtype=jnp.int32)
    flip, early, sy, sz = i // 32, (i // 16) % 2, (i // 4) % 4, i % 4
    half = jnp.where(early == 1, 1 - xl, xl)
    at = (half * 4 + ((y - sy) & 3)) * 4 + ((z - sz) & 3)
    return at * 2 + (core ^ flip)


def local(
    query_nope,
    query_rope,
    key_latent,
    key_rope,
    key_up,
    value_up,
    routed_tokens,
    expert_ids,
    expert_gates,
    gate_weight,
    up_weight,
    down_weight,
):
    outgoing, place_lo, place_hi = pack_rows(expert_ids.T, routed_tokens)
    outgoing, plane = plane_keys(key_latent, key_rope, outgoing)
    arrived = lax.all_to_all(outgoing, CHIPS, split_axis=0, concat_axis=0, tiled=True)
    gate = jnp.sum(jnp.where(expert_ids < NEXP, expert_gates, 0.0), axis=1, keepdims=True)
    gate_sib, up_sib = swap_core(gate_weight), swap_core(up_weight)
    wd_sib = swap_core(lax.optimization_barrier((down_weight, gate_sib))[0])
    early = to_second_half(lax.optimization_barrier((plane[0], up_sib))[0])
    arrived, plane, early = lax.optimization_barrier((arrived, plane, early))
    plane = jnp.concatenate(plane, axis=0)
    near, far = to_second_half(plane[4:10]), to_second_half(plane[10:], True)
    plane_sib = swap_core(plane)

    y = experts(arrived, gate_weight, gate_sib, up_weight, up_sib, down_weight, wd_sib)
    y, near, far, plane_sib = lax.optimization_barrier((y, near, far, plane_sib))
    pieces = [plane, early, near, far, plane_sib] + [swap_core(v) for v in (early, near, far)]
    pieces = lax.optimization_barrier((pieces, y))[0]
    returned = lax.all_to_all(y, CHIPS, split_axis=0, concat_axis=0, tiled=True)

    me = lax.axis_index(CTX).reshape(1).astype(jnp.int32)
    table = jnp.concatenate([me, key_places()])
    attention_out = attend(table, query_nope, query_rope, key_up, value_up, pieces)
    returned, attention_out = lax.optimization_barrier((returned, attention_out))

    routed_out = place_rows(returned, place_lo, place_hi, gate)
    return attention_out, routed_out


def solution(mesh):
    fine = Mesh(mesh.devices.reshape(2, 4, 2, 2, 2, 2), AXES)
    every = P(AXES)
    return jax.shard_map(
        local,
        mesh=fine,
        in_specs=(
            P(CTX, "sec"),
            P(CTX, "sec"),
            P(CTX, None),
            P(CTX, None),
            P("sec", None, None),
            P("sec", None, None),
            every,
            every,
            every,
            P(None, AXES),
            P(None, AXES),
            every,
        ),
        out_specs=(P(CTX, "sec"), every),
        check_vma=False,
    )
```

```python
import functools

import jax
import jax.numpy as jnp
from jax import lax
from jax.experimental import pallas as pl
from jax.experimental.pallas import tpu as pltpu
from jax.sharding import Mesh
from jax.sharding import PartitionSpec as P

AXES = ("xl", "y", "zh", "zl", "core", "sec")
CTX = ("xl", "y", "zh", "zl", "core")
CHIPS = ("xl", "y", "zh", "zl", "sec")
ROPE = 64
NOPE = 128
LAT = 512
KW = 640
CAP = 4
EB = 8
NEB = 2
SLOTS = 128
NEXP = 16
HALF = 3584
CB = 1792
NCB = HALF // CB
WB = 1792
NWB = HALF // WB
MB = 1024 * 1024
SMALL = 24 * MB
LARGE = 56 * MB
bf16 = jnp.bfloat16
f32 = jnp.float32


def swap_core(x):
    return lax.ppermute(x, "core", [(0, 1), (1, 0)])


def slot_select(ids, side):
    tokens = ids.shape[1]
    slot = lax.broadcasted_iota(jnp.int32, (SLOTS, tokens), 0)
    named = jnp.zeros((SLOTS, tokens), f32)
    for k in range(ids.shape[0]):
        named = named + jnp.where(ids[k : k + 1, :] == slot // 8, 1.0, 0.0)
    row_i = lax.broadcasted_iota(jnp.int32, (tokens, tokens), 0)
    col_i = lax.broadcasted_iota(jnp.int32, (tokens, tokens), 1)
    before = jnp.where(row_i < col_i, 1.0, 0.0).astype(bf16)
    rank = jnp.dot(named.astype(bf16), before, preferred_element_type=f32)
    hit = jnp.logical_and(named > 0.5, rank == (slot % 4).astype(f32))
    hit = jnp.logical_and(hit, (slot // 4) % 2 == side)
    return jnp.where(hit, 1.0, 0.0)


def pack_kernel(ids_ref, tok_lo, tok_hi, out_ref, place_lo, place_hi, sel_lo, sel_hi):
    @pl.when(pl.program_id(0) == 0)
    def _():
        for side, sel, place in ((0, sel_lo, place_lo), (1, sel_hi, place_hi)):
            chosen = slot_select(ids_ref[...], side)
            sel[...] = chosen.astype(bf16)
            place[...] = chosen.T.astype(bf16)

    rows = jnp.dot(sel_lo[...], tok_lo[...], preferred_element_type=f32)
    rows = rows + jnp.dot(sel_hi[...], tok_hi[...], preferred_element_type=f32)
    rows = rows.astype(bf16).reshape(NEXP, 1, 2 * CAP, CB)
    out_ref[...] = jnp.broadcast_to(rows, (NEXP, 4, 2 * CAP, CB)).reshape(4 * NEXP, 2 * CAP, CB)


def pack_rows(ids, tokens):
    n = tokens.shape[0]
    return pl.pallas_call(
        pack_kernel,
        grid=(NCB,),
        in_specs=[
            pl.BlockSpec((8, n), lambda i: (0, 0)),
            pl.BlockSpec((n, CB), lambda i: (0, i)),
            pl.BlockSpec((n, CB), lambda i: (0, NCB + i)),
        ],
        out_specs=[
            pl.BlockSpec((4 * NEXP, 2 * CAP, CB), lambda i: (0, 0, i)),
            pl.BlockSpec((n, SLOTS), lambda i: (0, 0)),
            pl.BlockSpec((n, SLOTS), lambda i: (0, 0)),
        ],
        out_shape=[
            jax.ShapeDtypeStruct((4 * NEXP, 2 * CAP, HALF), bf16),
            jax.ShapeDtypeStruct((n, SLOTS), bf16),
            jax.ShapeDtypeStruct((n, SLOTS), bf16),
        ],
        scratch_shapes=[pltpu.VMEM((SLOTS, n), bf16), pltpu.VMEM((SLOTS, n), bf16)],
        compiler_params=pltpu.CompilerParams(vmem_limit_bytes=LARGE),
        cost_estimate=pl.CostEstimate(flops=2 * 128 * 256 * HALF, bytes_accessed=6 * MB, transcendentals=0),
    )(ids, tokens, tokens)


def expert_kernel(x_ref, *rest):
    weights = rest[:8]
    downs = rest[8:12]
    out_ref, acc, hidden = rest[12:]
    step = pl.program_id(0)
    low = lax.broadcasted_iota(jnp.int32, (32, 8, WB), 1) < CAP

    def part(pair, fill):
        return jnp.where(low, pair, fill)

    @pl.when(step < NWB)
    def _():
        x = x_ref[...].astype(f32).reshape(32, 2, 8, WB)
        even, odd = x[:, 0], x[:, 1]
        x_lo = part(even, pltpu.roll(odd, CAP, 1)).reshape(256, WB).astype(bf16)
        x_hi = part(pltpu.roll(even, CAP, 1), odd).reshape(256, WB).astype(bf16)
        for i in range(4):
            cols = slice(i * 256, (i + 1) * 256)
            g = jnp.dot(x_lo, weights[2 * i][...], preferred_element_type=f32)
            g = g + jnp.dot(x_hi, weights[2 * i + 1][...], preferred_element_type=f32)
            acc[:, cols] = jnp.where(step == 0, g, acc[:, cols] + g)

    @pl.when(step == NWB - 1)
    def _():
        g, u = acc[:, :512], acc[:, 512:]
        hidden[...] = (g / (1.0 + jnp.exp(-g)) * u).astype(bf16)

    @pl.when(step >= NWB)
    def _():
        h_own, h_sib = hidden[:, :256], hidden[:, 256:]
        y = []
        for i in range(2):
            v = jnp.dot(h_own, downs[i][...], preferred_element_type=f32)
            v = v + jnp.dot(h_sib, downs[2 + i][...], preferred_element_type=f32)
            y.append(v.reshape(32, 8, WB))
        even = part(y[0], pltpu.roll(y[1], CAP, 1))
        odd = part(pltpu.roll(y[0], CAP, 1), y[1])
        out = jnp.concatenate([even[:, None], odd[:, None]], axis=1)
        out_ref[...] = out.reshape(64, 8, WB).astype(bf16)


def experts(x, gate, gate_sib, up, up_sib, wd, wd_sib):
    k = lambda i: jnp.minimum(i, NWB - 1)
    n = lambda i: jnp.maximum(i - NWB, 0)
    first = [pl.BlockSpec((WB, 256), lambda i: (k(i), 0)), pl.BlockSpec((WB, 256), lambda i: (NWB + k(i), 0))]
    second = [pl.BlockSpec((256, WB), lambda i: (0, n(i))), pl.BlockSpec((256, WB), lambda i: (0, NWB + n(i)))]
    return pl.pallas_call(
        expert_kernel,
        grid=(2 * NWB,),
        in_specs=[pl.BlockSpec((64, 8, WB), lambda i: (0, 0, k(i)))] + first * 4 + second * 2,
        out_specs=pl.BlockSpec((64, 8, WB), lambda i: (0, 0, n(i))),
        out_shape=jax.ShapeDtypeStruct((64, 8, HALF), bf16),
        scratch_shapes=[pltpu.VMEM((256, 1024), f32), pltpu.VMEM((256, 512), bf16)],
        compiler_params=pltpu.CompilerParams(vmem_limit_bytes=LARGE),
        cost_estimate=pl.CostEstimate(
            flops=2 * 256 * 7168 * 1536, bytes_accessed=30 * MB, transcendentals=256 * 512
        ),
    )(x, gate, gate, gate_sib, gate_sib, up, up, up_sib, up_sib, wd, wd, wd_sib, wd_sib)


def place_kernel(r_ref, sel_lo, sel_hi, gate_ref, out_ref, total):
    step = pl.program_id(0)

    @pl.when(step < NEB)
    def _():
        r = r_ref[...].reshape(EB, 4, 2 * CAP, HALF)
        rows = r[:, 0].astype(f32) + r[:, 1].astype(f32) + (r[:, 2].astype(f32) + r[:, 3].astype(f32))
        start = pl.multiple_of(step * EB * 2 * CAP, EB * 2 * CAP)
        total[pl.ds(start, EB * 2 * CAP), :] = rows.reshape(EB * 2 * CAP, HALF).astype(bf16)

    for side, sel in ((0, sel_lo), (1, sel_hi)):

        @pl.when(step == NEB + side)
        def _():
            rows = jnp.dot(sel[...], total[...], preferred_element_type=f32)
            out_ref[...] = (rows * gate_ref[...]).astype(bf16)


def place_rows(r, sel_lo, sel_hi, gate):
    n = gate.shape[0]
    full = lambda i: (0, 0)
    return pl.pallas_call(
        place_kernel,
        grid=(NEB + 2,),
        in_specs=[
            pl.BlockSpec((4 * EB, 2 * CAP, HALF), lambda i: (jnp.minimum(i, NEB - 1), 0, 0)),
            pl.BlockSpec((n, SLOTS), full),
            pl.BlockSpec((n, SLOTS), full),
            pl.BlockSpec((n, 1), full),
        ],
        out_specs=pl.BlockSpec((n, HALF), lambda i: (0, jnp.maximum(i - NEB, 0))),
        out_shape=jax.ShapeDtypeStruct((n, 2 * HALF), bf16),
        scratch_shapes=[pltpu.VMEM((SLOTS, HALF), bf16)],
        compiler_params=pltpu.CompilerParams(vmem_limit_bytes=SMALL),
        cost_estimate=pl.CostEstimate(flops=2 * 128 * 128 * 2 * HALF, bytes_accessed=6 * MB, transcendentals=0),
    )(r, sel_lo, sel_hi, gate)


GROUP = 16
PIECE = 256
KB = 2048


def query_kernel(nope_ref, rope_ref, ku_ref, q_ref):
    q_ref[:, LAT + ROPE :] = jnp.zeros((GROUP * 64, KW - LAT - ROPE), bf16)
    for h in range(GROUP):
        rows = pl.ds(h * 64, 64)
        q = lax.dot_general(
            nope_ref[:, h * NOPE : (h + 1) * NOPE], ku_ref[h], (((1,), (1,)), ((), ())), preferred_element_type=f32
        )
        q_ref[rows, :LAT] = q.astype(bf16)
        q_ref[rows, LAT : LAT + ROPE] = rope_ref[:, h * ROPE : (h + 1) * ROPE]


def queries(nope, rope, key_up):
    heads = key_up.shape[0]
    n = nope.shape[0]
    return pl.pallas_call(
        query_kernel,
        grid=(heads // GROUP,),
        in_specs=[
            pl.BlockSpec((n, GROUP * NOPE), lambda i: (0, i)),
            pl.BlockSpec((n, GROUP * ROPE), lambda i: (0, i)),
            pl.BlockSpec((GROUP, LAT, NOPE), lambda i: (i, 0, 0)),
        ],
        out_specs=pl.BlockSpec((GROUP * 64, KW), lambda i: (i, 0)),
        out_shape=jax.ShapeDtypeStruct((heads * 64, KW), bf16),
        compiler_params=pltpu.CompilerParams(vmem_limit_bytes=LARGE),
        cost_estimate=pl.CostEstimate(flops=2 * 64 * 32 * 128 * 512, bytes_accessed=8 * MB, transcendentals=0),
    )(nope, rope, key_up)


def attend_kernel(p_ref, q_ref, vu_ref, *rest):
    pieces = rest[:8]
    out_ref, keys, acc_ref, sems = rest[8:]
    me = p_ref[0]

    def copies():
        found = []
        for piece in pieces:
            for b in range(piece.shape[0]):
                n = len(found)
                start = pl.multiple_of(p_ref[1 + n] * 64, 64)
                found.append(pltpu.make_async_copy(piece.at[b], keys.at[pl.ds(start, 64), :], sems.at[n]))
        return found

    first = pl.program_id(0) == 0

    @pl.when(first)
    def _():
        for copy in copies():
            copy.start()

    @pl.when(first)
    def _():
        for copy in copies():
            copy.wait()

    scale = (NOPE + ROPE) ** -0.5 * 1.4426950408889634
    n_piece = GROUP * 64 // PIECE

    def score(j, i, masked):
        k = keys[pl.ds(pl.multiple_of(j * KB, KB), KB), :]
        q = q_ref[pl.ds(i * PIECE, PIECE), :]
        s = lax.dot_general(q, k, (((1,), (1,)), ((), ())), preferred_element_type=f32)
        if masked:
            key_place = j * KB + lax.broadcasted_iota(jnp.int32, (PIECE, KB), 1)
            place = me * 64 + lax.broadcasted_iota(jnp.int32, (PIECE, KB), 0) % 64
            s = jnp.where(key_place <= place, s, -1e30)
        return s

    def update(j, i, s, stat):
        m, l = stat
        rows = pl.ds(i * PIECE, PIECE)
        values = keys[pl.ds(pl.multiple_of(j * KB, KB), KB), :LAT]
        m_new = jnp.maximum(m, jnp.max(s, axis=1, keepdims=True))
        e = jnp.exp2(s * scale - m_new * scale)
        shrink = jnp.exp2((m - m_new) * scale)
        part = e[:, :128]
        for t in range(1, KB // 128):
            part = part + e[:, t * 128 : (t + 1) * 128]
        pv = jnp.dot(e.astype(bf16), values, preferred_element_type=f32)
        acc_ref[rows, :] = acc_ref[rows, :] * shrink + pv
        return m_new, l * shrink + part

    def chunk(j, stats, masked):
        s = score(j, 0, masked)
        fresh = []
        for i in range(n_piece):
            ahead = score(j, i + 1, masked) if i + 1 < n_piece else None
            fresh.append(update(j, i, s, stats[i]))
            s = ahead
        return tuple(fresh)

    acc_ref[...] = jnp.zeros_like(acc_ref)
    start = tuple(
        (jnp.full((PIECE, 1), -1e30, f32), jnp.zeros((PIECE, 128), f32)) for _ in range(n_piece)
    )
    last = me // (KB // 64)
    stats = chunk(last, start, True)
    stats = lax.fori_loop(0, last, lambda j, st: chunk(j, st, False), stats)
    for i in range(n_piece):
        rows = pl.ds(i * PIECE, PIECE)
        o = (acc_ref[rows, :] / jnp.sum(stats[i][1], axis=1, keepdims=True)).astype(bf16)
        for h in range(PIECE // 64):
            head = i * (PIECE // 64) + h
            v = jnp.dot(o[h * 64 : (h + 1) * 64, :], vu_ref[head], preferred_element_type=f32)
            out_ref[:, head * 128 : (head + 1) * 128] = v.astype(bf16)


def attend(places, query, value_up, pieces):
    heads = value_up.shape[0]
    n = query.shape[0] // heads
    return pl.pallas_call(
        attend_kernel,
        grid_spec=pltpu.PrefetchScalarGridSpec(
            num_scalar_prefetch=1,
            grid=(heads // GROUP,),
            in_specs=[
                pl.BlockSpec((GROUP * n, KW), lambda i, p: (i, 0)),
                pl.BlockSpec((GROUP, LAT, 128), lambda i, p: (i, 0, 0)),
            ]
            + [pl.BlockSpec(memory_space=pl.ANY)] * 8,
            out_specs=pl.BlockSpec((n, GROUP * 128), lambda i, p: (0, i)),
            scratch_shapes=[
                pltpu.VMEM((4096, KW), bf16),
                pltpu.VMEM((GROUP * 64, LAT), f32),
                pltpu.SemaphoreType.DMA((64,)),
            ],
        ),
        out_shape=jax.ShapeDtypeStruct((n, heads * 128), bf16),
        compiler_params=pltpu.CompilerParams(vmem_limit_bytes=LARGE),
        cost_estimate=pl.CostEstimate(
            flops=2 * 2048 * 4096 * 1152, bytes_accessed=12 * MB, transcendentals=2048 * 4096
        ),
    )(places, query, value_up, *pieces)


def ring(x, axis, step):
    return lax.ppermute(x, axis, [(i, (i + step) % 4) for i in range(4)])


Z_AXIS = ("zh", "zl")


def plane_keys(key_latent, key_rope, outgoing):
    n = key_latent.shape[0]
    own = jnp.concatenate([key_latent, key_rope, jnp.zeros((n, KW - LAT - ROPE), bf16)], axis=1)
    by_z = jnp.stack([own] + [ring(own, Z_AXIS, s) for s in (1, 2, 3)])
    outgoing, by_z = lax.optimization_barrier((outgoing, by_z))
    return outgoing, [by_z] + [ring(by_z, "y", s) for s in (1, 2, 3)]


def to_second_half(keys, far=False):
    return lax.ppermute(keys, ("xl", "sec"), [(0, 3), (1, 2)] if far else [(0, 2), (1, 3)])


def key_places():
    xl, y, core = lax.axis_index("xl"), lax.axis_index("y"), lax.axis_index("core")
    z = lax.axis_index(Z_AXIS)
    i = jnp.arange(64, dtype=jnp.int32)
    flip, early, sy, sz = i // 32, (i // 16) % 2, (i // 4) % 4, i % 4
    half = jnp.where(early == 1, 1 - xl, xl)
    at = (half * 4 + ((y - sy) & 3)) * 4 + ((z - sz) & 3)
    return at * 2 + (core ^ flip)


def local(
    query_nope,
    query_rope,
    key_latent,
    key_rope,
    key_up,
    value_up,
    routed_tokens,
    expert_ids,
    expert_gates,
    gate_weight,
    up_weight,
    down_weight,
):
    outgoing, place_lo, place_hi = pack_rows(expert_ids.T, routed_tokens)
    outgoing, plane = plane_keys(key_latent, key_rope, outgoing)
    arrived = lax.all_to_all(outgoing, CHIPS, split_axis=0, concat_axis=0, tiled=True)
    gate = jnp.sum(jnp.where(expert_ids < NEXP, expert_gates, 0.0), axis=1, keepdims=True)
    gate_sib, up_sib = swap_core(gate_weight), swap_core(up_weight)
    wd_sib = swap_core(lax.optimization_barrier((down_weight, gate_sib))[0])
    early = to_second_half(lax.optimization_barrier((plane[0], up_sib))[0])
    query = queries(query_nope, query_rope, key_up)
    arrived, plane, early, query = lax.optimization_barrier((arrived, plane, early, query))
    plane = jnp.concatenate(plane, axis=0)
    near, far = to_second_half(plane[4:10]), to_second_half(plane[10:], True)

    y = experts(arrived, gate_weight, gate_sib, up_weight, up_sib, down_weight, wd_sib)
    y, near, far = lax.optimization_barrier((y, near, far))
    pieces = [plane, early, near, far] + [swap_core(v) for v in (plane, early, near, far)]
    pieces = lax.optimization_barrier((pieces, y))[0]
    returned = lax.all_to_all(y, CHIPS, split_axis=0, concat_axis=0, tiled=True)

    me = lax.axis_index(CTX).reshape(1).astype(jnp.int32)
    table = jnp.concatenate([me, key_places()])
    attention_out = attend(table, query, value_up, pieces)
    returned, attention_out = lax.optimization_barrier((returned, attention_out))

    routed_out = place_rows(returned, place_lo, place_hi, gate)
    return attention_out, routed_out


def solution(mesh):
    fine = Mesh(mesh.devices.reshape(2, 4, 2, 2, 2, 2), AXES)
    every = P(AXES)
    return jax.shard_map(
        local,
        mesh=fine,
        in_specs=(
            P(CTX, "sec"),
            P(CTX, "sec"),
            P(CTX, None),
            P(CTX, None),
            P("sec", None, None),
            P("sec", None, None),
            every,
            every,
            every,
            P(None, AXES),
            P(None, AXES),
            every,
        ),
        out_specs=(P(CTX, "sec"), every),
        check_vma=False,
    )
```

```python
import functools

import jax
import jax.numpy as jnp
from jax import lax
from jax.experimental import pallas as pl
from jax.experimental.pallas import tpu as pltpu
from jax.sharding import Mesh
from jax.sharding import PartitionSpec as P

AXES = ("xl", "y", "zh", "zl", "core", "sec")
CTX = ("xl", "y", "zh", "zl", "core")
CHIPS = ("xl", "y", "zh", "zl", "sec")
ROPE = 64
NOPE = 128
LAT = 512
KW = 640
CAP = 4
EB = 8
NEB = 2
SLOTS = 128
NEXP = 16
HALF = 3584
CB = 1792
NCB = HALF // CB
WB = 1792
GB = 896
NGB = HALF // GB
NWB = HALF // WB
MB = 1024 * 1024
SMALL = 24 * MB
LARGE = 56 * MB
bf16 = jnp.bfloat16
f32 = jnp.float32


def swap_core(x):
    return lax.ppermute(x, "core", [(0, 1), (1, 0)])


def slot_select(ids, side):
    tokens = ids.shape[1]
    slot = lax.broadcasted_iota(jnp.int32, (SLOTS, tokens), 0)
    named = jnp.zeros((SLOTS, tokens), f32)
    for k in range(ids.shape[0]):
        named = named + jnp.where(ids[k : k + 1, :] == slot // 8, 1.0, 0.0)
    row_i = lax.broadcasted_iota(jnp.int32, (tokens, tokens), 0)
    col_i = lax.broadcasted_iota(jnp.int32, (tokens, tokens), 1)
    before = jnp.where(row_i < col_i, 1.0, 0.0).astype(bf16)
    rank = jnp.dot(named.astype(bf16), before, preferred_element_type=f32)
    hit = jnp.logical_and(named > 0.5, rank == (slot % 4).astype(f32))
    hit = jnp.logical_and(hit, (slot // 4) % 2 == side)
    return jnp.where(hit, 1.0, 0.0)


def pack_kernel(ids_ref, tok_lo, tok_hi, out_ref, place_lo, place_hi, sel_lo, sel_hi):
    @pl.when(pl.program_id(0) == 0)
    def _():
        for side, sel, place in ((0, sel_lo, place_lo), (1, sel_hi, place_hi)):
            chosen = slot_select(ids_ref[...], side)
            sel[...] = chosen.astype(bf16)
            place[...] = chosen.T.astype(bf16)

    rows = jnp.dot(sel_lo[...], tok_lo[...], preferred_element_type=f32)
    rows = rows + jnp.dot(sel_hi[...], tok_hi[...], preferred_element_type=f32)
    rows = rows.astype(bf16).reshape(NEXP, 1, 2 * CAP, CB)
    out_ref[...] = jnp.broadcast_to(rows, (NEXP, 4, 2 * CAP, CB)).reshape(4 * NEXP, 2 * CAP, CB)


def pack_rows(ids, tokens):
    n = tokens.shape[0]
    return pl.pallas_call(
        pack_kernel,
        grid=(NCB,),
        in_specs=[
            pl.BlockSpec((8, n), lambda i: (0, 0)),
            pl.BlockSpec((n, CB), lambda i: (0, i)),
            pl.BlockSpec((n, CB), lambda i: (0, NCB + i)),
        ],
        out_specs=[
            pl.BlockSpec((4 * NEXP, 2 * CAP, CB), lambda i: (0, 0, i)),
            pl.BlockSpec((n, SLOTS), lambda i: (0, 0)),
            pl.BlockSpec((n, SLOTS), lambda i: (0, 0)),
        ],
        out_shape=[
            jax.ShapeDtypeStruct((4 * NEXP, 2 * CAP, HALF), bf16),
            jax.ShapeDtypeStruct((n, SLOTS), bf16),
            jax.ShapeDtypeStruct((n, SLOTS), bf16),
        ],
        scratch_shapes=[pltpu.VMEM((SLOTS, n), bf16), pltpu.VMEM((SLOTS, n), bf16)],
        compiler_params=pltpu.CompilerParams(vmem_limit_bytes=LARGE),
        cost_estimate=pl.CostEstimate(flops=2 * 128 * 256 * HALF, bytes_accessed=6 * MB, transcendentals=0),
    )(ids, tokens, tokens)


def expert_kernel(x_ref, *rest):
    weights = rest[:8]
    downs = rest[8:12]
    out_ref, acc, hidden = rest[12:]
    step = pl.program_id(0)

    def part(pair, fill):
        return jnp.where(lax.broadcasted_iota(jnp.int32, pair.shape, 1) < CAP, pair, fill)

    @pl.when(step < NGB)
    def _():
        x = x_ref[...].astype(f32).reshape(32, 2, 8, GB)
        even, odd = x[:, 0], x[:, 1]
        x_lo = part(even, pltpu.roll(odd, CAP, 1)).reshape(256, GB).astype(bf16)
        x_hi = part(pltpu.roll(even, CAP, 1), odd).reshape(256, GB).astype(bf16)
        for i in range(4):
            cols = slice(i * 256, (i + 1) * 256)
            g = jnp.dot(x_lo, weights[2 * i][...], preferred_element_type=f32)
            g = g + jnp.dot(x_hi, weights[2 * i + 1][...], preferred_element_type=f32)
            acc[:, cols] = jnp.where(step == 0, g, acc[:, cols] + g)

    @pl.when(step == NGB - 1)
    def _():
        g, u = acc[:, :512], acc[:, 512:]
        hidden[...] = (g / (1.0 + jnp.exp(-g)) * u).astype(bf16)

    @pl.when(step >= NGB)
    def _():
        h_own, h_sib = hidden[:, :256], hidden[:, 256:]
        y = []
        for i in range(2):
            v = jnp.dot(h_own, downs[i][...], preferred_element_type=f32)
            v = v + jnp.dot(h_sib, downs[2 + i][...], preferred_element_type=f32)
            y.append(v.reshape(32, 8, WB))
        even = part(y[0], pltpu.roll(y[1], CAP, 1))
        odd = part(pltpu.roll(y[0], CAP, 1), y[1])
        out = jnp.concatenate([even[:, None], odd[:, None]], axis=1)
        out_ref[...] = out.reshape(64, 8, WB).astype(bf16)


def experts(x, gate, gate_sib, up, up_sib, wd, wd_sib):
    k = lambda i: jnp.minimum(i, NGB - 1)
    n = lambda i: jnp.maximum(i - NGB, 0)
    first = [pl.BlockSpec((GB, 256), lambda i: (k(i), 0)), pl.BlockSpec((GB, 256), lambda i: (NGB + k(i), 0))]
    second = [pl.BlockSpec((256, WB), lambda i: (0, n(i))), pl.BlockSpec((256, WB), lambda i: (0, NWB + n(i)))]
    return pl.pallas_call(
        expert_kernel,
        grid=(NGB + NWB,),
        in_specs=[pl.BlockSpec((64, 8, GB), lambda i: (0, 0, k(i)))] + first * 4 + second * 2,
        out_specs=pl.BlockSpec((64, 8, WB), lambda i: (0, 0, n(i))),
        out_shape=jax.ShapeDtypeStruct((64, 8, HALF), bf16),
        scratch_shapes=[pltpu.VMEM((256, 1024), f32), pltpu.VMEM((256, 512), bf16)],
        compiler_params=pltpu.CompilerParams(vmem_limit_bytes=LARGE),
        cost_estimate=pl.CostEstimate(
            flops=2 * 256 * 7168 * 1536, bytes_accessed=30 * MB, transcendentals=256 * 512
        ),
    )(x, gate, gate, gate_sib, gate_sib, up, up, up_sib, up_sib, wd, wd, wd_sib, wd_sib)


def place_kernel(r_ref, sel_lo, sel_hi, gate_ref, out_ref, total):
    step = pl.program_id(0)

    @pl.when(step < NEB)
    def _():
        r = r_ref[...].reshape(EB, 4, 2 * CAP, HALF)
        rows = r[:, 0].astype(f32) + r[:, 1].astype(f32) + (r[:, 2].astype(f32) + r[:, 3].astype(f32))
        start = pl.multiple_of(step * EB * 2 * CAP, EB * 2 * CAP)
        total[pl.ds(start, EB * 2 * CAP), :] = rows.reshape(EB * 2 * CAP, HALF).astype(bf16)

    for side, sel in ((0, sel_lo), (1, sel_hi)):

        @pl.when(step == NEB + side)
        def _():
            rows = jnp.dot(sel[...], total[...], preferred_element_type=f32)
            out_ref[...] = (rows * gate_ref[...]).astype(bf16)


def place_rows(r, sel_lo, sel_hi, gate):
    n = gate.shape[0]
    full = lambda i: (0, 0)
    return pl.pallas_call(
        place_kernel,
        grid=(NEB + 2,),
        in_specs=[
            pl.BlockSpec((4 * EB, 2 * CAP, HALF), lambda i: (jnp.minimum(i, NEB - 1), 0, 0)),
            pl.BlockSpec((n, SLOTS), full),
            pl.BlockSpec((n, SLOTS), full),
            pl.BlockSpec((n, 1), full),
        ],
        out_specs=pl.BlockSpec((n, HALF), lambda i: (0, jnp.maximum(i - NEB, 0))),
        out_shape=jax.ShapeDtypeStruct((n, 2 * HALF), bf16),
        scratch_shapes=[pltpu.VMEM((SLOTS, HALF), bf16)],
        compiler_params=pltpu.CompilerParams(vmem_limit_bytes=SMALL),
        cost_estimate=pl.CostEstimate(flops=2 * 128 * 128 * 2 * HALF, bytes_accessed=6 * MB, transcendentals=0),
    )(r, sel_lo, sel_hi, gate)


GROUP = 16
PIECE = 256
KB = 2048


def query_kernel(nope_ref, rope_ref, ku_ref, q_ref):
    q_ref[:, LAT + ROPE :] = jnp.zeros((GROUP * 64, KW - LAT - ROPE), bf16)
    for h in range(GROUP):
        rows = pl.ds(h * 64, 64)
        q = lax.dot_general(
            nope_ref[:, h * NOPE : (h + 1) * NOPE], ku_ref[h], (((1,), (1,)), ((), ())), preferred_element_type=f32
        )
        q_ref[rows, :LAT] = q.astype(bf16)
        q_ref[rows, LAT : LAT + ROPE] = rope_ref[:, h * ROPE : (h + 1) * ROPE]


def queries(nope, rope, key_up):
    heads = key_up.shape[0]
    n = nope.shape[0]
    return pl.pallas_call(
        query_kernel,
        grid=(heads // GROUP,),
        in_specs=[
            pl.BlockSpec((n, GROUP * NOPE), lambda i: (0, i)),
            pl.BlockSpec((n, GROUP * ROPE), lambda i: (0, i)),
            pl.BlockSpec((GROUP, LAT, NOPE), lambda i: (i, 0, 0)),
        ],
        out_specs=pl.BlockSpec((GROUP * 64, KW), lambda i: (i, 0)),
        out_shape=jax.ShapeDtypeStruct((heads * 64, KW), bf16),
        compiler_params=pltpu.CompilerParams(vmem_limit_bytes=LARGE),
        cost_estimate=pl.CostEstimate(flops=2 * 64 * 32 * 128 * 512, bytes_accessed=8 * MB, transcendentals=0),
    )(nope, rope, key_up)


def attend_kernel(p_ref, q_ref, vu_ref, *rest):
    pieces = rest[:8]
    out_ref, keys, acc_ref, sems = rest[8:]
    me = p_ref[0]

    def copies():
        found = []
        for piece in pieces:
            for b in range(piece.shape[0]):
                n = len(found)
                start = pl.multiple_of(p_ref[1 + n] * 64, 64)
                found.append(pltpu.make_async_copy(piece.at[b], keys.at[pl.ds(start, 64), :], sems.at[n]))
        return found

    first = pl.program_id(0) == 0

    @pl.when(first)
    def _():
        for copy in copies():
            copy.start()

    @pl.when(first)
    def _():
        for copy in copies():
            copy.wait()

    scale = (NOPE + ROPE) ** -0.5 * 1.4426950408889634
    n_piece = GROUP * 64 // PIECE

    def score(j, i, masked):
        k = keys[pl.ds(pl.multiple_of(j * KB, KB), KB), :]
        q = q_ref[pl.ds(i * PIECE, PIECE), :]
        s = lax.dot_general(q, k, (((1,), (1,)), ((), ())), preferred_element_type=f32)
        if masked:
            key_place = j * KB + lax.broadcasted_iota(jnp.int32, (PIECE, KB), 1)
            place = me * 64 + lax.broadcasted_iota(jnp.int32, (PIECE, KB), 0) % 64
            s = jnp.where(key_place <= place, s, -1e30)
        return s

    def update(j, i, s, stat):
        m, l = stat
        rows = pl.ds(i * PIECE, PIECE)
        values = keys[pl.ds(pl.multiple_of(j * KB, KB), KB), :LAT]
        m_new = jnp.maximum(m, jnp.max(s, axis=1, keepdims=True))
        e = jnp.exp2(s * scale - m_new * scale)
        shrink = jnp.exp2((m - m_new) * scale)
        part = e[:, :128]
        for t in range(1, KB // 128):
            part = part + e[:, t * 128 : (t + 1) * 128]
        pv = jnp.dot(e.astype(bf16), values, preferred_element_type=f32)
        acc_ref[rows, :] = acc_ref[rows, :] * shrink + pv
        return m_new, l * shrink + part

    def chunk(j, stats, masked):
        s = score(j, 0, masked)
        fresh = []
        for i in range(n_piece):
            ahead = score(j, i + 1, masked) if i + 1 < n_piece else None
            fresh.append(update(j, i, s, stats[i]))
            s = ahead
        return tuple(fresh)

    acc_ref[...] = jnp.zeros_like(acc_ref)
    start = tuple(
        (jnp.full((PIECE, 1), -1e30, f32), jnp.zeros((PIECE, 128), f32)) for _ in range(n_piece)
    )
    last = me // (KB // 64)
    stats = chunk(last, start, True)
    stats = lax.fori_loop(0, last, lambda j, st: chunk(j, st, False), stats)
    for i in range(n_piece):
        rows = pl.ds(i * PIECE, PIECE)
        o = (acc_ref[rows, :] / jnp.sum(stats[i][1], axis=1, keepdims=True)).astype(bf16)
        for h in range(PIECE // 64):
            head = i * (PIECE // 64) + h
            v = jnp.dot(o[h * 64 : (h + 1) * 64, :], vu_ref[head], preferred_element_type=f32)
            out_ref[:, head * 128 : (head + 1) * 128] = v.astype(bf16)


def attend(places, query, value_up, pieces):
    heads = value_up.shape[0]
    n = query.shape[0] // heads
    return pl.pallas_call(
        attend_kernel,
        grid_spec=pltpu.PrefetchScalarGridSpec(
            num_scalar_prefetch=1,
            grid=(heads // GROUP,),
            in_specs=[
                pl.BlockSpec((GROUP * n, KW), lambda i, p: (i, 0)),
                pl.BlockSpec((GROUP, LAT, 128), lambda i, p: (i, 0, 0)),
            ]
            + [pl.BlockSpec(memory_space=pl.ANY)] * 8,
            out_specs=pl.BlockSpec((n, GROUP * 128), lambda i, p: (0, i)),
            scratch_shapes=[
                pltpu.VMEM((4096, KW), bf16),
                pltpu.VMEM((GROUP * 64, LAT), f32),
                pltpu.SemaphoreType.DMA((64,)),
            ],
        ),
        out_shape=jax.ShapeDtypeStruct((n, heads * 128), bf16),
        compiler_params=pltpu.CompilerParams(vmem_limit_bytes=LARGE),
        cost_estimate=pl.CostEstimate(
            flops=2 * 2048 * 4096 * 1152, bytes_accessed=12 * MB, transcendentals=2048 * 4096
        ),
    )(places, query, value_up, *pieces)


def ring(x, axis, step):
    return lax.ppermute(x, axis, [(i, (i + step) % 4) for i in range(4)])


Z_AXIS = ("zh", "zl")


def plane_keys(key_latent, key_rope, outgoing):
    n = key_latent.shape[0]
    own = jnp.concatenate([key_latent, key_rope, jnp.zeros((n, KW - LAT - ROPE), bf16)], axis=1)
    by_z = jnp.stack([own] + [ring(own, Z_AXIS, s) for s in (1, 2, 3)])
    outgoing, by_z = lax.optimization_barrier((outgoing, by_z))
    return outgoing, [by_z] + [ring(by_z, "y", s) for s in (1, 2, 3)]


def to_second_half(keys, far=False):
    return lax.ppermute(keys, ("xl", "sec"), [(0, 3), (1, 2)] if far else [(0, 2), (1, 3)])


def key_places():
    xl, y, core = lax.axis_index("xl"), lax.axis_index("y"), lax.axis_index("core")
    z = lax.axis_index(Z_AXIS)
    i = jnp.arange(64, dtype=jnp.int32)
    flip, early, sy, sz = i // 32, (i // 16) % 2, (i // 4) % 4, i % 4
    half = jnp.where(early == 1, 1 - xl, xl)
    at = (half * 4 + ((y - sy) & 3)) * 4 + ((z - sz) & 3)
    return at * 2 + (core ^ flip)


def local(
    query_nope,
    query_rope,
    key_latent,
    key_rope,
    key_up,
    value_up,
    routed_tokens,
    expert_ids,
    expert_gates,
    gate_weight,
    up_weight,
    down_weight,
):
    outgoing, place_lo, place_hi = pack_rows(expert_ids.T, routed_tokens)
    outgoing, plane = plane_keys(key_latent, key_rope, outgoing)
    arrived = lax.all_to_all(outgoing, CHIPS, split_axis=0, concat_axis=0, tiled=True)
    gate = jnp.sum(jnp.where(expert_ids < NEXP, expert_gates, 0.0), axis=1, keepdims=True)
    gate_sib, up_sib = swap_core(gate_weight), swap_core(up_weight)
    wd_sib = swap_core(lax.optimization_barrier((down_weight, gate_sib))[0])
    early = to_second_half(lax.optimization_barrier((plane[0], up_sib))[0])
    query = queries(query_nope, query_rope, key_up)
    arrived, plane, early, query = lax.optimization_barrier((arrived, plane, early, query))
    plane = jnp.concatenate(plane, axis=0)
    near, far = to_second_half(plane[4:10]), to_second_half(plane[10:], True)

    y = experts(arrived, gate_weight, gate_sib, up_weight, up_sib, down_weight, wd_sib)
    y, near, far = lax.optimization_barrier((y, near, far))
    pieces = [plane, early, near, far] + [swap_core(v) for v in (plane, early, near, far)]
    pieces = lax.optimization_barrier((pieces, y))[0]
    returned = lax.all_to_all(y, CHIPS, split_axis=0, concat_axis=0, tiled=True)

    me = lax.axis_index(CTX).reshape(1).astype(jnp.int32)
    table = jnp.concatenate([me, key_places()])
    attention_out = attend(table, query, value_up, pieces)
    returned, attention_out = lax.optimization_barrier((returned, attention_out))

    routed_out = place_rows(returned, place_lo, place_hi, gate)
    return attention_out, routed_out


def solution(mesh):
    fine = Mesh(mesh.devices.reshape(2, 4, 2, 2, 2, 2), AXES)
    every = P(AXES)
    return jax.shard_map(
        local,
        mesh=fine,
        in_specs=(
            P(CTX, "sec"),
            P(CTX, "sec"),
            P(CTX, None),
            P(CTX, None),
            P("sec", None, None),
            P("sec", None, None),
            every,
            every,
            every,
            P(None, AXES),
            P(None, AXES),
            every,
        ),
        out_specs=(P(CTX, "sec"), every),
        check_vma=False,
    )
```
